512 devices in a mesh: tm: 8 (over y, core), row: 16 (over z), col: 4 (over x).
Axes of the slice: x: 4, y: 4, z: 16, core: 2. Of those that a mesh axis runs over, the one named last changes fastest.
Arguments:
- right_side: float32 [3, 8, 512, 1024], P(None, 'tm', 'row', 'col'), may hold values from -6 to 6
- seam_mask: int32 [8, 512, 1024], P('tm', 'row', 'col'), may hold values 0 or 1
- patch_inverse: float32 [1024, 1024], replicated, may hold values from -0.5 to 1.5, as said below
- row_coupling: float32 [32, 32], replicated, may hold values from -0.5 to 1.5, as said below
- col_coupling: float32 [64, 64], replicated, may hold values from -0.5 to 1.5, as said below
Outputs:
- solution: float32 [3, 8, 512, 1024], P(None, 'tm', 'row', 'col')
The draws below stay inside these ranges and needn't reach their ends.
Inputs may be any that keep to these rules, and one draw needn't show every extreme that they name: `patch_inverse`: symmetric and positive definite. `row_coupling`: symmetric and positive definite. `col_coupling`: symmetric and positive definite.
All inputs are finite; a program needn't handle non-finite values. No bound on the sum of `seam_mask` on one device may be relied on, other than what follows from the above.
Results may differ from the reference program's by a relative error of at most 0.0015.
Values sent between devices are 32-bit elements; how exact they have to be, the bound alone decides.
No kernel may reach another device: no remote copies, remote signals or barrier semaphores. Data moves between devices by JAX's collectives and lax.ppermute only.
A program may use at most 64 MiB of HBM per device.

```python
import math
import jax
import jax.numpy as jnp
from jax import lax

CHANNELS = 3
PATCH = 32
COARSE = 16
ITERS = 2
CORE = 16
OVER = 8
FRAMES = 8
HEIGHT = 512
WIDTH = 1024
CROWS = 32
CCOLS = 64


def symmetric_dominant(key, order, scale):
    diag_key, noise_key = jax.random.split(key)
    diagonal = jax.random.uniform(diag_key, (order,), jnp.float32, 1.0, 1.5)
    noise = jax.random.truncated_normal(noise_key, -4.0, 4.0, (order, order), jnp.float32)
    spread = 0.3 / math.sqrt(order) / math.sqrt(2.0)
    off_part = (noise + noise.T) * spread * (1.0 - jnp.eye(order, dtype=jnp.float32))
    return scale * (jnp.diag(diagonal) + off_part)


def draw_patch_inverse(key, part):
    key = jax.random.fold_in(key, 31)
    return symmetric_dominant(key, PATCH * PATCH, 1.0)


def draw_row_coupling(key, part):
    key = jax.random.fold_in(key, 32)
    return symmetric_dominant(key, CROWS, 0.6)


def draw_col_coupling(key, part):
    key = jax.random.fold_in(key, 33)
    return symmetric_dominant(key, CCOLS, 0.3)


def touch_ends(result, rng, smallest, largest):
    longest = result.shape.index(max(result.shape))
    spots = []
    for shift in (0, 1):
        where = [jax.random.randint(jax.random.fold_in(rng, axis), (), 0, length) for axis, length in enumerate(result.shape)]
        where[longest] = (where[longest] + shift) % result.shape[longest]
        spots.append(tuple(where))
    return result.at[spots[0]].set(smallest).at[spots[1]].set(largest)


def level_of(stream_key, shape, cuts, least, top_value):
    factor_of, own = 1.0, jax.random.fold_in(stream_key, 6)
    for position, blocks in cuts:
        draws = jnp.exp(jax.random.uniform(jax.random.fold_in(own, position), (blocks,), jnp.float32, least / len(cuts), top_value / len(cuts)))
        factor_of = factor_of * jnp.repeat(draws, shape[position] // blocks).reshape([-1 if axis == position else 1 for axis in range(len(shape))])
    return factor_of


def centred(own_key, extent, scale, limit, cuts=(), kind=jnp.bfloat16):
    array = scale * jax.random.normal(own_key, extent, jnp.float32)
    if cuts:
        array = array * level_of(own_key, extent, cuts, -0.22, 0.18)
    return jnp.clip(array, -limit, limit).astype(kind)


def setup_inputs(seed: int = 0) -> dict:
    keys = jax.random.split(jax.random.key(seed), 6)
    return {
        "right_side": centred(keys[0], (CHANNELS, FRAMES, HEIGHT, WIDTH), 1.0, 6.0, ((1, 8), (2, 16), (3, 4)), jnp.float32),
        "seam_mask": touch_ends((jax.random.randint(keys[1], (FRAMES, HEIGHT, WIDTH), 0, 4) < 1).astype(jnp.int32), jax.random.fold_in(keys[1], 1), 0, 1),
        "patch_inverse": draw_patch_inverse(jax.random.fold_in(keys[5], 71), 0),
        "row_coupling": draw_row_coupling(jax.random.fold_in(keys[5], 71), 0),
        "col_coupling": draw_col_coupling(jax.random.fold_in(keys[5], 71), 0),
    }


seam_screen = 0.1
keep_screen = 2.0
time_coupling = 1.0
highest = lax.Precision.HIGHEST


def operate(values, seam_mask):
    screen = jnp.where(seam_mask == 1, seam_screen, keep_screen).astype(jnp.float32)
    padded = jnp.pad(values, ((0, 0), (1, 1), (1, 1), (1, 1)))
    in_plane = padded[:, 1:-1, 2:, 1:-1] + padded[:, 1:-1, :-2, 1:-1] + padded[:, 1:-1, 1:-1, 2:] + padded[:, 1:-1, 1:-1, :-2]
    across = padded[:, 2:, 1:-1, 1:-1] + padded[:, :-2, 1:-1, 1:-1]
    return (screen + 4.0 + 2.0 * time_coupling) * values - in_plane - time_coupling * across


def patch_sums(extended, inverse, core_size, patch_keep):
    channels, frames, ext_rows, ext_cols = extended.shape
    row_blocks = ext_rows // core_size
    col_blocks = ext_cols // core_size
    blocks = extended.reshape(channels, frames, row_blocks, core_size, col_blocks, core_size)
    row_pairs = jnp.concatenate([blocks[:, :, :-1], blocks[:, :, 1:]], axis=3)
    both_pairs = jnp.concatenate([row_pairs[:, :, :, :, :-1], row_pairs[:, :, :, :, 1:]], axis=5)
    flattened = both_pairs.transpose(0, 1, 2, 4, 3, 5).reshape(-1, 4 * core_size * core_size)
    solved = jnp.dot(flattened, inverse, precision=highest, preferred_element_type=jnp.float32)
    solved = solved.reshape(channels, frames, row_blocks - 1, col_blocks - 1, 2 * core_size, 2 * core_size)
    solved = solved * patch_keep[None, None, :, :, None, None]
    solved = solved.transpose(0, 1, 2, 4, 3, 5)
    zero_rows = jnp.zeros((channels, frames, 1, core_size, col_blocks - 1, 2 * core_size), jnp.float32)
    row_sums = jnp.concatenate([solved[:, :, :, :core_size], zero_rows], axis=2) + jnp.concatenate([zero_rows, solved[:, :, :, core_size:]], axis=2)
    zero_cols = jnp.zeros((channels, frames, row_blocks, core_size, 1, core_size), jnp.float32)
    col_sums = jnp.concatenate([row_sums[..., :core_size], zero_cols], axis=4) + jnp.concatenate([zero_cols, row_sums[..., core_size:]], axis=4)
    return col_sums.reshape(channels, frames, ext_rows, ext_cols)


def coarse_fix(residual, row_coupling, col_coupling):
    channels, frames, height, width = residual.shape
    coarse_sum = residual.reshape(channels, frames, height // COARSE, COARSE, width // COARSE, COARSE).sum(axis=(3, 5))
    half_done = jnp.einsum('cfjk,lk->cfjl', coarse_sum, col_coupling, precision=highest)
    coarse_done = jnp.einsum('ij,cfjl->cfil', row_coupling, half_done, precision=highest)
    spread = jnp.broadcast_to(coarse_done[:, :, :, None, :, None], (channels, frames, height // COARSE, COARSE, width // COARSE, COARSE))
    return spread.reshape(residual.shape)


def precondition(residual, patch_inverse, row_coupling, col_coupling):
    padded = jnp.pad(residual, ((0, 0), (0, 0), (OVER, OVER), (OVER, OVER)))
    patch_keep = jnp.ones((HEIGHT // CORE, WIDTH // CORE), jnp.float32)

    def per_channel(channel_field):
        return patch_sums(channel_field[None], patch_inverse, CORE, patch_keep)[0]

    spread = lax.map(per_channel, padded)
    local = spread[:, :, OVER:OVER + HEIGHT, OVER:OVER + WIDTH]
    return local + coarse_fix(residual, row_coupling, col_coupling)


def reference(right_side, seam_mask, patch_inverse, row_coupling, col_coupling):
    solution = jnp.zeros_like(right_side)
    residual = right_side
    precond = precondition(residual, patch_inverse, row_coupling, col_coupling)
    direction = precond
    inner_now = jnp.sum(residual * precond)
    for iteration in range(ITERS):
        image = operate(direction, seam_mask)
        step_size = inner_now / jnp.sum(direction * image)
        solution = solution + step_size * direction
        if iteration + 1 < ITERS:
            residual = residual - step_size * image
            precond = precondition(residual, patch_inverse, row_coupling, col_coupling)
            inner_next = jnp.sum(residual * precond)
            direction = precond + (inner_next / inner_now) * direction
            inner_now = inner_next
    return solution
```

```python
import jax
import jax.numpy as jnp
from jax import lax
from jax.sharding import PartitionSpec as P

COARSE = 16
CORE = 16
OVER = 8


seam_screen = 0.1
keep_screen = 2.0
time_coupling = 1.0
highest = lax.Precision.HIGHEST


def with_halo(block, sides, width):
    for axis, dim in sides:
        count = lax.axis_size(axis)
        forward = [(i, i + 1) for i in range(count - 1)]
        backward = [(target, source) for source, target in forward]
        low = lax.ppermute(
            lax.slice_in_dim(block, block.shape[dim] - width, None, axis=dim), axis, forward
        )
        high = lax.ppermute(lax.slice_in_dim(block, 0, width, axis=dim), axis, backward)
        block = jnp.concatenate([low, block, high], axis=dim)
    return block


def operate(values, seam_mask):
    screen = jnp.where(seam_mask == 1, seam_screen, keep_screen).astype(jnp.float32)
    low_row, high_row = shifted(values[:, :, -1:], values[:, :, :1], "row")
    low_col, high_col = shifted(values[:, :, :, -1:], values[:, :, :, :1], "col")
    before, after = shifted(values, values, "tm")
    rows = jnp.concatenate([low_row, values, high_row], axis=2)
    cols = jnp.concatenate([low_col, values, high_col], axis=3)
    in_plane = rows[:, :, 2:] + rows[:, :, :-2] + cols[:, :, :, 2:] + cols[:, :, :, :-2]
    across = before + after
    return (screen + 4.0 + 2.0 * time_coupling) * values - in_plane - time_coupling * across


def shifted(last, first, axis):
    count = lax.axis_size(axis)
    forward = [(i, i + 1) for i in range(count - 1)]
    backward = [(target, source) for source, target in forward]
    return lax.ppermute(last, axis, forward), lax.ppermute(first, axis, backward)


def patch_sums(extended, inverse, core_size):
    channels, frames, ext_rows, ext_cols = extended.shape
    row_blocks = ext_rows // core_size
    col_blocks = ext_cols // core_size
    blocks = extended.reshape(channels, frames, row_blocks, core_size, col_blocks, core_size)
    row_pairs = jnp.concatenate([blocks[:, :, :-1], blocks[:, :, 1:]], axis=3)
    both_pairs = jnp.concatenate([row_pairs[:, :, :, :, :-1], row_pairs[:, :, :, :, 1:]], axis=5)
    flattened = both_pairs.transpose(0, 1, 2, 4, 3, 5).reshape(-1, 4 * core_size * core_size)
    solved = jnp.dot(flattened, inverse, precision=lax.Precision.HIGH, preferred_element_type=jnp.float32)
    solved = solved.reshape(
        channels, frames, row_blocks - 1, col_blocks - 1, 2 * core_size, 2 * core_size
    )
    solved = solved.transpose(0, 1, 2, 4, 3, 5)
    zero_rows = jnp.zeros(
        (channels, frames, 1, core_size, col_blocks - 1, 2 * core_size), jnp.float32
    )
    row_sums = jnp.concatenate([solved[:, :, :, :core_size], zero_rows], axis=2) + jnp.concatenate(
        [zero_rows, solved[:, :, :, core_size:]], axis=2
    )
    zero_cols = jnp.zeros((channels, frames, row_blocks, core_size, 1, core_size), jnp.float32)
    col_sums = jnp.concatenate([row_sums[..., :core_size], zero_cols], axis=4) + jnp.concatenate(
        [zero_cols, row_sums[..., core_size:]], axis=4
    )
    return col_sums.reshape(channels, frames, ext_rows, ext_cols)


def fold_rim(received, along, extent, margin):
    center = lax.slice_in_dim(received, 2 * margin, 2 * margin + extent, axis=along)
    upper = lax.slice_in_dim(received, 0, margin, axis=along)
    lower = lax.slice_in_dim(received, extent + 3 * margin, extent + 4 * margin, axis=along)
    upper_pad = tuple(
        ((0, extent - margin) if position == along else (0, 0) for position in range(received.ndim))
    )
    lower_pad = tuple(
        ((extent - margin, 0) if position == along else (0, 0) for position in range(received.ndim))
    )
    return center + jnp.pad(upper, upper_pad) + jnp.pad(lower, lower_pad)


def everyone(value, axes):
    count = lax.axis_size(axes)
    copies = jnp.broadcast_to(value[None], (count,) + value.shape)
    return lax.all_to_all(copies, axes, 0, 0)


def coarse_fix(residual, row_coupling, col_coupling):
    channels, frames, height, width = residual.shape
    coarse_rows = height // COARSE
    coarse_cols = width // COARSE
    coarse_sum = residual.reshape(channels, frames, coarse_rows, COARSE, coarse_cols, COARSE).sum(
        axis=(3, 5)
    )
    rows = lax.axis_size("row")
    cols = lax.axis_size("col")
    gathered = everyone(coarse_sum, ("row", "col"))
    all_grid = gathered.reshape(rows, cols, channels, frames, coarse_rows, coarse_cols)
    all_grid = all_grid.transpose(2, 3, 0, 4, 1, 5).reshape(
        channels, frames, rows * coarse_rows, cols * coarse_cols
    )
    col_start = lax.axis_index("col") * coarse_cols
    own_cols = lax.dynamic_slice_in_dim(col_coupling, col_start, coarse_cols, axis=0)
    row_start = lax.axis_index("row") * coarse_rows
    own_rows = lax.dynamic_slice_in_dim(row_coupling, row_start, coarse_rows, axis=0)
    half_done = jnp.einsum("cfjk,lk->cfjl", all_grid, own_cols, precision=highest)
    coarse_done = jnp.einsum("ij,cfjl->cfil", own_rows, half_done, precision=highest)
    spread = jnp.broadcast_to(
        coarse_done[:, :, :, None, :, None],
        (channels, frames, coarse_rows, COARSE, coarse_cols, COARSE),
    )
    return spread.reshape(residual.shape)


def precondition(residual, patch_inverse, row_coupling, col_coupling):
    height = residual.shape[2]
    width = residual.shape[3]
    extended = with_halo(residual, (("row", 2), ("col", 3)), OVER)
    spread = patch_sums(extended, patch_inverse, CORE)
    received = with_halo(spread, (("row", 2), ("col", 3)), OVER)
    local = fold_rim(fold_rim(received, 2, height, OVER), 3, width, OVER)
    return local + coarse_fix(residual, row_coupling, col_coupling)


def shards(right_side, seam_mask, patch_inverse, row_coupling, col_coupling):
    first = precondition(right_side, patch_inverse, row_coupling, col_coupling)
    image = operate(first, seam_mask)
    second = precondition(image, patch_inverse, row_coupling, col_coupling)
    second_image = operate(second, seam_mask)
    pairs = jnp.stack([
        jnp.sum(right_side * first),
        jnp.sum(first * image),
        jnp.sum(image * second),
        jnp.sum(second * second_image),
    ])
    pairs = jnp.sum(everyone(pairs, ("tm", "col")), axis=0)
    pairs = jnp.sum(everyone(pairs, "row"), axis=0)
    inner0, curve0, cross, curve_second = pairs[0], pairs[1], pairs[2], pairs[3]
    step0 = inner0 / curve0
    inner1 = inner0 - 2.0 * step0 * curve0 + step0 * step0 * cross
    grow = 1.0 + inner1 / inner0
    curve1 = grow * grow * curve0 - 2.0 * grow * step0 * cross + step0 * step0 * curve_second
    step1 = inner1 / curve1
    return (step0 + step1 * grow) * first - (step1 * step0) * second


def solution(mesh):
    in_specs = (P(None, "tm", "row", "col"), P("tm", "row", "col"), P(), P(), P())
    out_specs = P(None, "tm", "row", "col")
    return jax.shard_map(shards, mesh=mesh, in_specs=in_specs, out_specs=out_specs, check_vma=False)
```

```python
import functools

import jax
import jax.numpy as jnp
from jax import lax
from jax.experimental import pallas as pl
from jax.experimental.pallas import tpu as pltpu
from jax.sharding import PartitionSpec as P

CELL = 16
RIM = 24
seam_screen = 0.1
keep_screen = 2.0
highest = lax.Precision.HIGHEST
f32 = jnp.float32
bf16 = jnp.bfloat16

ROWS = 32
COLS = 256
TALL = ROWS + 2 * RIM
LANES = 384
PATCH_ROWS = 16
PATCH_COLS = 18
PATCHES = PATCH_ROWS * PATCH_COLS
FLAT = 272
SPREAD = 96


def call(body, outs, scratch=(), limit=40):
    shapes = [jax.ShapeDtypeStruct(shape, f32) for shape in outs]
    return pl.pallas_call(
        body,
        out_shape=shapes,
        scratch_shapes=list(scratch),
        compiler_params=pltpu.CompilerParams(vmem_limit_bytes=limit * 1024 * 1024),
    )


def lanes_of(shape):
    return lax.broadcasted_iota(jnp.int32, shape, len(shape) - 1)


def rows_of(ref, start, count):
    return jnp.concatenate([ref[group, pl.ds(start, count), :] for group in range(3)], axis=1)


def put_rows(ref, start, count, value):
    for group in range(3):
        ref[group, pl.ds(start, count), :] = value[:, 128 * group : 128 * group + 128]


def stripe_of(ref, start):
    return jnp.concatenate([ref.at[group][pl.ds(start, PATCH_ROWS, stride=CELL), :] for group in range(3)], axis=1)


def swap_blocks(parts):
    lane = lanes_of(parts[0].shape)
    for step in (1, 2):
        taken = (lane // (32 * step)) % 2 == 1
        fresh = list(parts)
        for low in range(4):
            if low & step:
                continue
            first, second = parts[low], parts[low + step]
            fresh[low] = jnp.where(taken, pltpu.roll(second, 32 * step, 1), first)
            fresh[low + step] = jnp.where(taken, second, pltpu.roll(first, 128 - 32 * step, 1))
        parts = fresh
    return parts


def patch_apply(field, result, high_w, low_w, keep, high_x, low_x, solved):
    for block in range(8):
        slabs = [stripe_of(field, 4 * block + row) for row in range(4)]
        for parity in range(2):
            if parity:
                slabs = [pltpu.roll(slab, LANES - CELL, 1) for slab in slabs]
            for group in range(3):
                parts = swap_blocks([slab[:, 128 * group : 128 * group + 128] for slab in slabs])
                for inner in range(4):
                    place = 8 * group + 2 * inner + parity
                    if place >= PATCH_COLS:
                        continue
                    upper = parts[inner].astype(bf16)
                    lower = (parts[inner] - upper.astype(f32)).astype(bf16)
                    where = (pl.ds(PATCH_ROWS * place, PATCH_ROWS), pl.ds(128 * block, 128))
                    high_x[where] = upper
                    low_x[where] = lower
    for part in range(4):
        span = pl.ds(256 * part, 256)
        dot = functools.partial(jnp.dot, preferred_element_type=f32)
        total = dot(high_x[...], high_w[:, span]) + dot(high_x[...], low_w[:, span])
        total = total + dot(low_x[...], high_w[:, span])
        solved[:, span] = total * keep[...]
    put_rows(result, FLAT - CELL, CELL, jnp.zeros((CELL, LANES), f32))
    for block in range(8):
        sums = None
        for parity in range(2):
            slabs = [[] for _ in range(4)]
            for group in range(3):
                parts = []
                for inner in range(4):
                    place = 8 * group + 2 * inner + parity
                    if place >= PATCH_COLS:
                        parts.append(jnp.zeros((PATCH_ROWS, 128), f32))
                    else:
                        parts.append(solved[pl.ds(PATCH_ROWS * place, PATCH_ROWS), pl.ds(128 * block, 128)])
                for row, piece in enumerate(swap_blocks(parts)):
                    slabs[row].append(piece)
            wide = [jnp.concatenate(pieces, axis=1) for pieces in slabs]
            if parity:
                sums = [total + pltpu.roll(slab, CELL, 1) for total, slab in zip(sums, wide)]
            else:
                sums = wide
        for row in range(4):
            total = sums[row]
            if block >= 4:
                total = total + stripe_of(result, 4 * block + row)
            for group in range(3):
                spot = pl.ds(4 * block + row, PATCH_ROWS, stride=CELL)
                result.at[group][spot, :] = total[:, 128 * group : 128 * group + 128]


def merge_sides(middle, left, right):
    lane = lanes_of(left.shape)
    first = jnp.where(lane < RIM, left, middle[:, :128])
    last = jnp.where((lane >= RIM) & (lane < 2 * RIM), right, middle[:, 256:])
    return jnp.concatenate([first, middle[:, 128:256], last], axis=1)


def cell_sums(blocks):
    rows = [jnp.sum(block[CELL * half : CELL * half + CELL], axis=0, keepdims=True) for block in blocks for half in range(2)]
    lane = lax.broadcasted_iota(jnp.int32, (LANES, 128), 0) - RIM
    cell = lanes_of((LANES, 128))
    inside = (lane >= CELL * cell) & (lane < CELL * cell + CELL) & (cell < COLS // CELL)
    stacked = jnp.concatenate(rows, axis=0)
    return jnp.dot(stacked, inside.astype(f32), precision=highest, preferred_element_type=f32)


def assemble(low, block, mask, high, tall, to_right, to_left, cells):
    own = []
    for channel in range(4):
        if channel < 3:
            middle = block[channel]
        else:
            middle = jnp.where(mask[...] == 1, seam_screen, keep_screen).astype(f32)
        column = jnp.concatenate([low[channel], middle, high[channel]], axis=0)
        wide = jnp.concatenate([column, jnp.zeros((TALL, 128), f32)], axis=1)
        wide = pltpu.roll(wide, RIM, 1)
        tall[channel] = wide
        to_right[channel] = wide[:, 256:]
        to_left[channel] = wide[:, :128]
        own.append(wide[RIM : RIM + ROWS])
    cells[...] = cell_sums(own)


def first_apply(tall, left, right, cells, high_w, low_w, keep, result, screen, share, field, high_x, low_x, solved):
    put_rows(field, 240, FLAT - 240, jnp.zeros((FLAT - 240, LANES), f32))
    for channel in range(3):
        put_rows(field, TALL * channel, TALL, merge_sides(tall[channel], left[channel], right[channel]))
    screen[...] = merge_sides(tall[3], left[3], right[3])
    patch_apply(field, result, high_w, low_w, keep, high_x, low_x, solved)
    for channel in range(3):
        share[pl.ds(ROWS * channel, ROWS), :] = rows_of(result, TALL * channel + RIM, ROWS)
    share[pl.ds(3 * ROWS, 8), :] = jnp.concatenate([cells[...], jnp.zeros((8, 256), f32)], axis=1)


def first_image(result, before, after, screen, cells, image, message):
    lane = lanes_of((ROWS, LANES))
    own = (lane >= RIM) & (lane < RIM + COLS)
    blocks = []
    for channel in range(3):
        base = TALL * channel + RIM
        center = rows_of(result, base, ROWS)
        near = rows_of(result, base - 1, ROWS) + rows_of(result, base + 1, ROWS)
        near = near + pltpu.roll(center, 1, 1) + pltpu.roll(center, LANES - 1, 1)
        span = pl.ds(ROWS * channel, ROWS)
        value = (screen[pl.ds(RIM, ROWS), :] + 6.0) * center - near - before[span, :] - after[span, :]
        value = jnp.where(own, value, 0.0)
        image[channel] = value
        blocks.append(value)
    sums = cell_sums(blocks)
    beside = before[pl.ds(3 * ROWS, 8), :128] + after[pl.ds(3 * ROWS, 8), :128]
    rows = [cells[0:6], beside[0:6], sums, cells[6:8]]
    rows = [part[row : row + 1] for part in rows for row in range(part.shape[0])]
    lane = lanes_of((1, 128))
    packed = []
    for group in range(3):
        total = jnp.zeros((1, 128), f32)
        for spot in range(8):
            if 8 * group + spot < len(rows):
                row = rows[8 * group + spot]
                row = pltpu.roll(row, CELL * spot, 1) if spot else row
                total = jnp.where(lane // CELL == spot, row, total)
        packed.append(total)
    message[...] = jnp.concatenate(packed, axis=1)


def second_apply(
    row_count, col_count, place, gathered, block, result, image, low, high, left, right, screen, high_w, low_w, keep,
    row_mix, col_mix, row_spread, col_spread, first, second, partial,
    field, output, high_x, low_x, solved, coarse, beside, letters,
):
    dot = functools.partial(jnp.dot, precision=highest, preferred_element_type=f32)
    lane = lanes_of((row_count, 128))
    put_rows(letters, 0, row_count * col_count, gathered[...])

    def grid_of(index):
        halves = []
        for half in range(2):
            chunk = 2 * index + half
            total = jnp.zeros((row_count, 128), f32)
            for col in range(col_count):
                piece = letters.at[chunk // 8][pl.ds(col, row_count, stride=col_count), :]
                shift = (CELL * col - CELL * (chunk % 8)) % 128
                piece = pltpu.roll(piece, shift, 1) if shift else piece
                total = jnp.where(lane // CELL == col, piece, total)
            halves.append(total)
        return jnp.concatenate(halves, axis=0)

    def spread(grid):
        return dot(row_spread[...], dot(grid, col_spread[...]))

    screen_cells = grid_of(9)
    grid_lane = lanes_of((2 * row_count, 128))
    zero_row = jnp.zeros((1, 128), f32)
    row0 = 2 * place[0] * CELL - RIM
    col0 = place[1] * COLS - RIM
    tall_row = lax.broadcasted_iota(jnp.int32, (TALL, LANES), 0) + row0
    tall_col = lanes_of((TALL, LANES))
    real = tall_col < COLS + 2 * RIM
    tall_col = tall_col + col0
    inside = (tall_row >= 0) & (tall_row < ROWS * row_count) & (tall_col >= 0) & (tall_col < COLS * col_count) & real
    tall_lane = lanes_of((ROWS, LANES))
    own = (tall_lane >= RIM) & (tall_lane < RIM + COLS)
    put_rows(field, 240, FLAT - 240, jnp.zeros((FLAT - 240, LANES), f32))
    first_grids = []
    for channel in range(3):
        sums = grid_of(channel)
        beside_sums = grid_of(3 + channel)
        level = dot(dot(row_mix[...], sums), col_mix[...])
        level_beside = dot(dot(row_mix[...], beside_sums), col_mix[...])
        even, odd = level[:row_count], level[row_count:]
        above = jnp.concatenate([zero_row, odd[:-1], even], axis=0)
        below = jnp.concatenate([odd, even[1:], zero_row], axis=0)
        before = jnp.where(grid_lane == 0, 0.0, pltpu.roll(level, 1, 1))
        after = jnp.where(grid_lane == CELL * col_count - 1, 0.0, pltpu.roll(level, 127, 1))
        image_sums = grid_of(6 + channel) + (screen_cells + 576.0) * level
        image_sums = image_sums - 16.0 * (above + below + before + after) - 256.0 * level_beside
        first_grids.append(image_sums)
        coarse[channel] = spread(sums)
        beside[channel] = spread(beside_sums)
    for channel in range(3):
        center = coarse[channel, pl.ds(8, TALL), :]
        near = coarse[channel, pl.ds(7, TALL), :] + coarse[channel, pl.ds(9, TALL), :]
        near = near + pltpu.roll(center, 1, 1) + pltpu.roll(center, LANES - 1, 1)
        value = (screen[...] + 6.0) * center - near - beside[channel, pl.ds(8, TALL), :]
        middle = jnp.concatenate([low[channel], image[channel], high[channel]], axis=0)
        value = value + merge_sides(middle, left[channel], right[channel])
        put_rows(field, TALL * channel, TALL, jnp.where(inside, value, 0.0))
    patch_apply(field, output, high_w, low_w, keep, high_x, low_x, solved)
    totals = [jnp.zeros((ROWS, LANES), f32) for _ in range(4)]
    for channel in range(3):
        whole = rows_of(output, TALL * channel, TALL) + spread(first_grids[channel])[8 : 8 + TALL]
        put_rows(output, TALL * channel, TALL, jnp.where(inside, whole, 0.0))
        base = TALL * channel + RIM
        new = rows_of(output, base, ROWS)
        near = rows_of(output, base - 1, ROWS) + rows_of(output, base + 1, ROWS)
        near = near + pltpu.roll(new, 1, 1) + pltpu.roll(new, LANES - 1, 1)
        new_image = (screen[pl.ds(RIM, ROWS), :] + 6.0) * new - near
        old = jnp.where(own, rows_of(result, base, ROWS) + coarse[channel, pl.ds(8 + RIM, ROWS), :], 0.0)
        new = jnp.where(own, new, 0.0)
        old_image = rows_of(field, base, ROWS)
        totals[0] = totals[0] + block[channel, pl.ds(RIM, ROWS), :] * old
        totals[1] = totals[1] + old * old_image
        totals[2] = totals[2] + old_image * new
        totals[3] = totals[3] + new * new_image
        first[pl.ds(ROWS * channel, ROWS), :] = pltpu.roll(old, LANES - RIM, 1)[:, :COLS]
        second[pl.ds(ROWS * channel, ROWS), :] = pltpu.roll(new, LANES - RIM, 1)[:, :COLS]
    lane = lanes_of((1, 128))
    packed = jnp.zeros((1, 128), f32)
    for index, total in enumerate(totals):
        value = jnp.sum(jnp.sum(total, axis=0, keepdims=True), axis=1, keepdims=True)
        packed = jnp.where(lane == index, value, packed)
    partial[...] = packed


def couple(copies, second, before, partial, shared):
    product = second[...] * before[...]
    value = jnp.sum(jnp.sum(product, axis=0, keepdims=True), axis=1, keepdims=True)
    packed = partial[...] - jnp.where(lanes_of((1, 128)) == 3, 2.0 * value, 0.0)
    shared[...] = jnp.broadcast_to(packed[None], (copies, 1, 128))


def regroup(copies, received, shared):
    total = jnp.sum(received[...], axis=0, keepdims=True)
    shared[...] = jnp.broadcast_to(total, (copies, 1, 128))


def combine(received, first, second, solution_block):
    total = jnp.sum(received[...], axis=0)
    lane = lanes_of((1, 128))
    inner0, curve0, cross, curve_second = [
        jnp.sum(jnp.where(lane == index, total, 0.0), axis=1, keepdims=True) for index in range(4)
    ]
    step0 = inner0 / curve0
    inner1 = inner0 - 2.0 * step0 * curve0 + step0 * step0 * cross
    grow = 1.0 + inner1 / inner0
    curve1 = grow * grow * curve0 - 2.0 * grow * step0 * cross + step0 * step0 * curve_second
    step1 = inner1 / curve1
    solution_block[...] = (step0 + step1 * grow) * first[...] - (step1 * step0) * second[...]


def exchange(last, first, axis):
    count = lax.axis_size(axis)
    forward = [(i, i + 1) for i in range(count - 1)]
    backward = [(target, source) for source, target in forward]
    return lax.ppermute(last, axis, forward), lax.ppermute(first, axis, backward)


def shards(right_side, seam_mask, patch_inverse, row_coupling, col_coupling):
    frame_count, row_count, col_count = (lax.axis_size(axis) for axis in ("tm", "row", "col"))
    own_row, own_col = lax.axis_index("row"), lax.axis_index("col")
    block = right_side[:, 0]
    mask = seam_mask[0]
    screen_edge = jnp.where(seam_mask == 1, seam_screen, keep_screen).astype(f32)
    edge = jnp.concatenate([block, screen_edge], axis=0)
    low, high = exchange(edge[:, ROWS - RIM :], edge[:, :RIM], "row")

    rounded = lax.reduce_precision(patch_inverse, 8, 7)
    high_w = rounded.astype(bf16)
    low_w = (patch_inverse - rounded).astype(bf16)
    index = jnp.arange(PATCHES)
    kind = index % PATCH_ROWS
    patch_row = 2 * own_row + kind % 5 - 1
    patch_col = 16 * own_col + index // PATCH_ROWS - 1
    keep = (kind < 15) & (kind % 5 < 4) & (patch_row >= 0) & (patch_row < 2 * row_count)
    keep = keep & (patch_col >= 0) & (patch_col < 16 * col_count)
    keep = keep.astype(f32)[:, None]
    coarse_rows, coarse_cols = 2 * row_count, 16 * col_count
    row_of = 2 * own_row + (jnp.arange(SPREAD) - ROWS) // CELL
    lane_col = jnp.arange(LANES) - RIM
    lane_col = jnp.where(lane_col >= 320, lane_col - LANES, lane_col)
    col_of = 16 * own_col + lane_col // CELL
    row_pick = (row_of[:, None] == jnp.arange(coarse_rows)[None]).astype(f32)
    col_pick = (jnp.arange(coarse_cols)[:, None] == col_of[None]).astype(f32)
    swapped = row_coupling.reshape(coarse_rows, row_count, 2).transpose(0, 2, 1).reshape(coarse_rows, coarse_rows)
    row_spread = jnp.dot(row_pick, swapped, precision=highest)
    row_mix = swapped.reshape(row_count, 2, coarse_rows).transpose(1, 0, 2).reshape(coarse_rows, coarse_rows)
    col_turned = jnp.pad(col_coupling.T, ((0, 128 - coarse_cols), (0, 128 - coarse_cols)))
    col_spread = jnp.dot(col_turned[:, :coarse_cols], col_pick, precision=highest)
    place = jnp.stack([own_row, own_col]).astype(jnp.int32)

    tall, to_right, to_left, cells = call(
        assemble, [(4, TALL, LANES), (4, TALL, 128), (4, TALL, 128), (8, 128)]
    )(low, block, mask, high)
    left, right = exchange(to_right, to_left, "col")
    work = [
        pltpu.VMEM((PATCHES, 1024), bf16),
        pltpu.VMEM((PATCHES, 1024), bf16),
        pltpu.VMEM((PATCHES, 1024), f32),
    ]
    result, screen, share = call(
        first_apply,
        [(3, FLAT, 128), (TALL, LANES), (3 * ROWS + 8, LANES)],
        [pltpu.VMEM((3, FLAT, 128), f32)] + work,
    )(tall, left, right, cells, high_w, low_w, keep)
    before, after = exchange(share, share, "tm")
    image, message = call(first_image, [(3, ROWS, LANES), (1, LANES)])(result, before, after, screen, cells)
    low, high = exchange(image[:, ROWS - RIM :], image[:, :RIM], "row")
    peers = row_count * col_count
    gathered = lax.all_to_all(jnp.broadcast_to(message[None], (peers, 1, LANES)), ("row", "col"), 0, 0)
    gathered = gathered.reshape(peers, LANES)
    column = jnp.concatenate([low, image, high], axis=1)
    left, right = exchange(column[:, :, 256:], column[:, :, :128], "col")
    plain = pl.BlockSpec(memory_space=pltpu.VMEM)
    first, second, partial = pl.pallas_call(
        functools.partial(second_apply, row_count, col_count),
        out_shape=[
            jax.ShapeDtypeStruct((3 * ROWS, COLS), f32),
            jax.ShapeDtypeStruct((3 * ROWS, COLS), f32),
            jax.ShapeDtypeStruct((1, 128), f32),
        ],
        in_specs=[pl.BlockSpec(memory_space=pltpu.SMEM)] + [plain] * 16,
        out_specs=[plain] * 3,
        scratch_shapes=[pltpu.VMEM((3, FLAT, 128), f32)] * 2
        + work
        + [pltpu.VMEM((3, SPREAD, LANES), f32)] * 2
        + [pltpu.VMEM((3, peers, 128), f32)],
        compiler_params=pltpu.CompilerParams(vmem_limit_bytes=40 * 1024 * 1024),
    )(
        place, gathered, tall, result, image, low, high, left, right, screen, high_w, low_w, keep,
        row_mix, col_turned, row_spread, col_spread,
    )
    forward = [(i, i + 1) for i in range(frame_count - 1)]
    previous = lax.ppermute(second, "tm", forward)
    group = frame_count * col_count
    (shared,) = call(functools.partial(couple, group), [(group, 1, 128)])(second, previous, partial)
    received = lax.all_to_all(shared, ("tm", "col"), 0, 0)
    (shared,) = call(functools.partial(regroup, row_count), [(row_count, 1, 128)])(received)
    received = lax.all_to_all(shared, "row", 0, 0)
    (answer,) = call(combine, [(3 * ROWS, COLS)])(received, first, second)
    return answer.reshape(right_side.shape)


def solution(mesh):
    in_specs = (P(None, "tm", "row", "col"), P("tm", "row", "col"), P(), P(), P())
    out_specs = P(None, "tm", "row", "col")
    return jax.shard_map(shards, mesh=mesh, in_specs=in_specs, out_specs=out_specs, check_vma=False)
```

```python
import functools

import jax
import jax.numpy as jnp
from jax import lax
from jax.experimental import pallas as pl
from jax.experimental.pallas import tpu as pltpu
from jax.sharding import PartitionSpec as P

CELL = 16
RIM = 24
SIDE = 56
seam_screen = 0.1
keep_screen = 2.0
highest = lax.Precision.HIGHEST
f32 = jnp.float32
bf16 = jnp.bfloat16

ROWS = 32
COLS = 256
TALL = ROWS + 2 * RIM
LANES = 384
PATCH_ROWS = 16
PATCH_COLS = 22
PATCHES = PATCH_ROWS * PATCH_COLS
FLAT = 272
SPREAD = 96


def call(body, outs, kinds, scratch=(), limit=8):
    specs = [pl.BlockSpec(memory_space=pltpu.SMEM) if kind == "s" else pl.BlockSpec() for kind in kinds]
    return pl.pallas_call(
        body,
        out_shape=[jax.ShapeDtypeStruct(shape, f32) for shape in outs],
        in_specs=specs,
        scratch_shapes=list(scratch),
        compiler_params=pltpu.CompilerParams(vmem_limit_bytes=limit * 1024 * 1024),
    )


def lanes_of(shape):
    return lax.broadcasted_iota(jnp.int32, shape, len(shape) - 1)


def rows_of(ref, start, count):
    return jnp.concatenate([ref[group, pl.ds(start, count), :] for group in range(3)], axis=1)


def put_rows(ref, start, count, value):
    for group in range(3):
        ref[group, pl.ds(start, count), :] = value[:, 128 * group : 128 * group + 128]


def stripe_of(ref, start):
    return jnp.concatenate([ref.at[group][pl.ds(start, PATCH_ROWS, stride=CELL), :] for group in range(3)], axis=1)


def swap_blocks(parts):
    lane = lanes_of(parts[0].shape)
    for step in (1, 2):
        taken = (lane // (32 * step)) % 2 == 1
        fresh = list(parts)
        for low in range(4):
            if low & step:
                continue
            first, second = parts[low], parts[low + step]
            fresh[low] = jnp.where(taken, pltpu.roll(second, 32 * step, 1), first)
            fresh[low + step] = jnp.where(taken, second, pltpu.roll(first, 128 - 32 * step, 1))
        parts = fresh
    return parts


def patch_apply(span_of, field, result, inverse, high_w, low_w, keep, high_x, low_x, solved):
    start, stop = span_of
    used = pl.ds(0, PATCH_ROWS * (stop - start))

    for block in range(8):
        slabs = [stripe_of(field, 4 * block + row) for row in range(4)]
        for parity in range(2):
            if parity:
                slabs = [pltpu.roll(slab, LANES - CELL, 1) for slab in slabs]
            for group in range(3):
                parts = swap_blocks([slab[:, 128 * group : 128 * group + 128] for slab in slabs])
                for inner in range(4):
                    place = 8 * group + 2 * inner + parity
                    if not start <= place < stop:
                        continue
                    upper = parts[inner].astype(bf16)
                    lower = (parts[inner] - upper.astype(f32)).astype(bf16)
                    where = (pl.ds(PATCH_ROWS * (place - start), PATCH_ROWS), pl.ds(128 * block, 128))
                    high_x[where] = upper
                    low_x[where] = lower
    for part in range(16):
        span = pl.ds(64 * part, 64)
        upper = inverse[span, :].astype(bf16)
        high_w[span, :] = upper
        low_w[span, :] = (inverse[span, :] - upper.astype(f32)).astype(bf16)
    for part in range(4):
        span = pl.ds(256 * part, 256)
        dot = functools.partial(jnp.dot, preferred_element_type=f32)
        total = dot(high_x[used, :], high_w[:, span]) + dot(high_x[used, :], low_w[:, span])
        total = total + dot(low_x[used, :], high_w[:, span])
        solved[used, span] = total * keep[pl.ds(PATCH_ROWS * start, PATCH_ROWS * (stop - start)), :]
    put_rows(result, FLAT - CELL, CELL, jnp.zeros((CELL, LANES), f32))
    for block in range(8):
        sums = None
        for parity in range(2):
            slabs = [[] for _ in range(4)]
            for group in range(3):
                parts = []
                for inner in range(4):
                    place = 8 * group + 2 * inner + parity
                    if not start <= place < stop:
                        parts.append(jnp.zeros((PATCH_ROWS, 128), f32))
                    else:
                        parts.append(solved[pl.ds(PATCH_ROWS * (place - start), PATCH_ROWS), pl.ds(128 * block, 128)])
                for row, piece in enumerate(swap_blocks(parts)):
                    slabs[row].append(piece)
            wide = [jnp.concatenate(pieces, axis=1) for pieces in slabs]
            if parity:
                sums = [total + pltpu.roll(slab, CELL, 1) for total, slab in zip(sums, wide)]
            else:
                sums = wide
        for row in range(4):
            total = sums[row]
            if block >= 4:
                total = total + stripe_of(result, 4 * block + row)
            for group in range(3):
                spot = pl.ds(4 * block + row, PATCH_ROWS, stride=CELL)
                result.at[group][spot, :] = total[:, 128 * group : 128 * group + 128]


def inside_of(place, row_count, col_count, rim):
    row = lax.broadcasted_iota(jnp.int32, (TALL, LANES), 0) + (place[0] * ROWS - RIM)
    lane = lanes_of((TALL, LANES))
    col = lane + (place[1] * COLS - SIDE)
    near = (lane >= SIDE - rim) & (lane < SIDE + COLS + rim)
    return (row >= 0) & (row < ROWS * row_count) & (col >= 0) & (col < COLS * col_count) & near


def merge_sides(middle, left, right):
    lane = lanes_of(left.shape)
    first = jnp.where(lane < SIDE, left, middle[:, :128])
    last = jnp.where((lane >= SIDE) & (lane < 2 * SIDE), right, middle[:, 256:])
    return jnp.concatenate([first, middle[:, 128:256], last], axis=1)


def cell_sums(blocks):
    rows = [jnp.sum(block[CELL * half : CELL * half + CELL], axis=0, keepdims=True) for block in blocks for half in range(2)]
    lane = lax.broadcasted_iota(jnp.int32, (LANES, 128), 0) - SIDE
    cell = lanes_of((LANES, 128))
    inside = (lane >= CELL * cell) & (lane < CELL * cell + CELL) & (cell < COLS // CELL)
    stacked = jnp.concatenate(rows, axis=0)
    return jnp.dot(stacked, inside.astype(f32), precision=highest, preferred_element_type=f32)


def assemble(low, block, mask, high, tall, to_right, to_left, cells):
    own = []
    for channel in range(4):
        if channel < 3:
            middle = block[channel]
        else:
            middle = jnp.where(mask[...] == 1, seam_screen, keep_screen).astype(f32)
        column = jnp.concatenate([low[channel], middle, high[channel]], axis=0)
        wide = jnp.concatenate([column, jnp.zeros((TALL, 128), f32)], axis=1)
        wide = pltpu.roll(wide, SIDE, 1)
        tall[channel] = wide
        to_right[channel] = wide[:, 256:]
        to_left[channel] = wide[:, :128]
        own.append(wide[RIM : RIM + ROWS])
    cells[...] = cell_sums(own)


def prepare(row_count, col_count, place, row_coupling, col_coupling, row_mix, row_spread, col_mix, col_spread, keep):
    dot = functools.partial(jnp.dot, precision=highest, preferred_element_type=f32)
    turned = functools.partial(
        lax.dot_general, dimension_numbers=(((1,), (1,)), ((), ())), precision=highest, preferred_element_type=f32
    )
    coarse_rows, coarse_cols = 2 * row_count, CELL * col_count

    def matrix(shape, rule):
        return rule(lax.broadcasted_iota(jnp.int32, shape, 0), lanes_of(shape)).astype(f32)

    order = matrix((coarse_rows, coarse_rows), lambda i, j: (j // 2 == i % row_count) & (j % 2 == i // row_count))
    swapped = turned(row_coupling[...], order)
    row_mix[...] = dot(order, swapped)
    row_pick = matrix((SPREAD, coarse_rows), lambda i, j: (i + place[0] * ROWS - ROWS + CELL * 2) // CELL - 2 == j)
    row_spread[...] = dot(row_pick, swapped)
    col_turned = turned(matrix((128, coarse_cols), lambda i, j: i == j), col_coupling[...])
    col_mix[...] = dot(col_turned, matrix((coarse_cols, 128), lambda i, j: i == j))

    def column(cell, lane):
        col = lane + (place[1] * COLS - SIDE)
        return (col >= CELL * cell) & (col < CELL * cell + CELL)

    col_spread[...] = dot(col_turned, matrix((coarse_cols, LANES), column))
    index = lax.broadcasted_iota(jnp.int32, (PATCHES, 1), 0)
    kind = index % PATCH_ROWS
    patch_row = 2 * place[0] + kind % 5 - 1
    patch_col = CELL * place[1] + index // PATCH_ROWS - 3
    kept = (kind < 15) & (kind % 5 < 4) & (patch_row >= 0) & (patch_row < coarse_rows)
    keep[...] = (kept & (patch_col >= 0) & (patch_col < coarse_cols)).astype(f32)


def edges(block, mask, last, first):
    for channel in range(3):
        last[channel] = block[channel, ROWS - RIM :]
        first[channel] = block[channel, :RIM]
    screen = jnp.where(mask[...] == 1, seam_screen, keep_screen).astype(f32)
    last[3] = screen[ROWS - RIM :]
    first[3] = screen[:RIM]


def first_apply(
    row_count, col_count, place, tall, left, right, cells, inverse, keep, result, screen, share,
    field, high_x, low_x, solved, high_w, low_w,
):
    put_rows(field, 240, FLAT - 240, jnp.zeros((FLAT - 240, LANES), f32))
    for channel in range(3):
        put_rows(field, TALL * channel, TALL, merge_sides(tall[channel], left[channel], right[channel]))
    screen[...] = merge_sides(tall[3], left[3], right[3])
    patch_apply((0, PATCH_COLS), field, result, inverse, high_w, low_w, keep, high_x, low_x, solved)
    inside = inside_of(place, row_count, col_count, 40)
    for channel in range(3):
        whole = rows_of(result, TALL * channel, TALL)
        put_rows(result, TALL * channel, TALL, jnp.where(inside, whole, 0.0))
        share[pl.ds(ROWS * channel, ROWS), :] = rows_of(result, TALL * channel + RIM, ROWS)
    share[pl.ds(3 * ROWS, 8), :] = jnp.concatenate([cells[...], jnp.zeros((8, 256), f32)], axis=1)


def first_image(copies, row_count, col_count, place, result, before, after, screen, cells, image, last, first, message):
    inside = inside_of(place, row_count, col_count, RIM)[RIM : RIM + ROWS]
    blocks = []
    for channel in range(3):
        base = TALL * channel + RIM
        center = rows_of(result, base, ROWS)
        near = rows_of(result, base - 1, ROWS) + rows_of(result, base + 1, ROWS)
        near = near + pltpu.roll(center, 1, 1) + pltpu.roll(center, LANES - 1, 1)
        span = pl.ds(ROWS * channel, ROWS)
        value = (screen[pl.ds(RIM, ROWS), :] + 6.0) * center - near - before[span, :] - after[span, :]
        value = jnp.where(inside, value, 0.0)
        image[channel] = value
        last[channel] = value[ROWS - RIM :]
        first[channel] = value[:RIM]
        blocks.append(value)
    sums = cell_sums(blocks)
    beside = before[pl.ds(3 * ROWS, 8), :128] + after[pl.ds(3 * ROWS, 8), :128]
    rows = [cells[0:6], beside[0:6], sums, cells[6:8]]
    rows = [part[row : row + 1] for part in rows for row in range(part.shape[0])]
    lane = lanes_of((1, 128))
    packed = []
    for group in range(3):
        total = jnp.zeros((1, 128), f32)
        for spot in range(8):
            if 8 * group + spot < len(rows):
                row = rows[8 * group + spot]
                row = pltpu.roll(row, CELL * spot, 1) if spot else row
                total = jnp.where(lane // CELL == spot, row, total)
        packed.append(total)
    message[...] = jnp.broadcast_to(jnp.concatenate(packed, axis=1)[None], (copies, 1, LANES))


def second_apply(
    row_count, col_count, place, gathered, block, result, image, low, high, screen, inverse,
    keep, row_mix, col_mix, row_spread, col_spread, first, second, partial,
    field, output, high_x, low_x, solved, high_w, low_w, coarse, beside, late, letters,
):
    dot = functools.partial(jnp.dot, precision=highest, preferred_element_type=f32)
    coarse_rows = 2 * row_count
    lane = lanes_of((row_count, 128))
    for group in range(3):
        letters[group] = gathered[:, 0, 128 * group : 128 * group + 128]

    def grid_of(index):
        halves = []
        for half in range(2):
            chunk = 2 * index + half
            total = jnp.zeros((row_count, 128), f32)
            for col in range(col_count):
                piece = letters.at[chunk // 8][pl.ds(col, row_count, stride=col_count), :]
                shift = (CELL * col - CELL * (chunk % 8)) % 128
                piece = pltpu.roll(piece, shift, 1) if shift else piece
                total = jnp.where(lane // CELL == col, piece, total)
            halves.append(total)
        return jnp.concatenate(halves, axis=0)

    def beside_each_other(tall, width):
        count = tall.shape[0] // coarse_rows
        return jnp.concatenate([tall[coarse_rows * i : coarse_rows * (i + 1)] for i in range(count)], axis=1)

    def spread(tall, targets):
        wide = dot(row_spread[...], beside_each_other(dot(tall, col_spread[...]), LANES))
        for index, (ref, channel) in enumerate(targets):
            ref[channel] = wide[:, LANES * index : LANES * (index + 1)]

    screen_cells = grid_of(9)
    grid_lane = lanes_of((coarse_rows, 128))
    zero_row = jnp.zeros((1, 128), f32)
    inside = inside_of(place, row_count, col_count, RIM)
    tall_lane = lanes_of((ROWS, LANES))
    own = (tall_lane >= SIDE) & (tall_lane < SIDE + COLS)
    put_rows(field, 240, FLAT - 240, jnp.zeros((FLAT - 240, LANES), f32))
    sums = jnp.concatenate([grid_of(index) for index in range(6)], axis=0)
    spread(sums, [(coarse, 0), (coarse, 1), (coarse, 2), (beside, 0), (beside, 1), (beside, 2)])
    for channel in range(3):
        center = coarse[channel, pl.ds(8, TALL), :]
        near = coarse[channel, pl.ds(7, TALL), :] + coarse[channel, pl.ds(9, TALL), :]
        near = near + pltpu.roll(center, 1, 1) + pltpu.roll(center, LANES - 1, 1)
        value = (screen[...] + 6.0) * center - near - beside[channel, pl.ds(8, TALL), :]
        middle = jnp.concatenate([low[channel], image[channel], high[channel]], axis=0)
        value = value + middle
        put_rows(field, TALL * channel, TALL, jnp.where(inside, value, 0.0))
    levels = dot(row_mix[...], beside_each_other(dot(sums, col_mix[...]), 128))
    late_sums = []
    for channel in range(3):
        level = levels[:, 128 * channel : 128 * channel + 128]
        level_beside = levels[:, 384 + 128 * channel : 512 + 128 * channel]
        even, odd = level[:row_count], level[row_count:]
        above = jnp.concatenate([zero_row, odd[:-1], even], axis=0)
        below = jnp.concatenate([odd, even[1:], zero_row], axis=0)
        before = jnp.where(grid_lane == 0, 0.0, pltpu.roll(level, 1, 1))
        after = jnp.where(grid_lane == CELL * col_count - 1, 0.0, pltpu.roll(level, 127, 1))
        image_sums = grid_of(6 + channel) + (screen_cells + 576.0) * level
        late_sums.append(image_sums - 16.0 * (above + below + before + after) - 256.0 * level_beside)
    spread(jnp.concatenate(late_sums, axis=0), [(late, 0), (late, 1), (late, 2)])
    patch_apply((2, PATCH_COLS - 2), field, output, inverse, high_w, low_w, keep, high_x, low_x, solved)
    totals = [jnp.zeros((ROWS, LANES), f32) for _ in range(4)]
    for channel in range(3):
        whole = rows_of(output, TALL * channel, TALL) + late[channel, pl.ds(8, TALL), :]
        put_rows(output, TALL * channel, TALL, jnp.where(inside, whole, 0.0))
        base = TALL * channel + RIM
        new = rows_of(output, base, ROWS)
        near = rows_of(output, base - 1, ROWS) + rows_of(output, base + 1, ROWS)
        near = near + pltpu.roll(new, 1, 1) + pltpu.roll(new, LANES - 1, 1)
        new_image = (screen[pl.ds(RIM, ROWS), :] + 6.0) * new - near
        old = jnp.where(own, rows_of(result, base, ROWS) + coarse[channel, pl.ds(8 + RIM, ROWS), :], 0.0)
        new = jnp.where(own, new, 0.0)
        old_image = jnp.where(own, rows_of(field, base, ROWS), 0.0)
        totals[0] = totals[0] + block[channel, pl.ds(RIM, ROWS), :] * old
        totals[1] = totals[1] + old * old_image
        totals[2] = totals[2] + old_image * new
        totals[3] = totals[3] + new * new_image
        first[pl.ds(ROWS * channel, ROWS), :] = pltpu.roll(old, LANES - SIDE, 1)[:, :COLS]
        second[pl.ds(ROWS * channel, ROWS), :] = pltpu.roll(new, LANES - SIDE, 1)[:, :COLS]
    lane = lanes_of((1, 128))
    packed = jnp.zeros((1, 128), f32)
    for index, total in enumerate(totals):
        value = jnp.sum(jnp.sum(total, axis=0, keepdims=True), axis=1, keepdims=True)
        packed = jnp.where(lane == index, value, packed)
    partial[...] = packed


def couple(copies, second, before, partial, shared):
    product = second[...] * before[...]
    value = jnp.sum(jnp.sum(product, axis=0, keepdims=True), axis=1, keepdims=True)
    packed = partial[...] - jnp.where(lanes_of((1, 128)) == 3, 2.0 * value, 0.0)
    shared[...] = jnp.broadcast_to(packed[None], (copies, 1, 128))


def regroup(copies, received, shared):
    total = jnp.sum(received[...], axis=0, keepdims=True)
    shared[...] = jnp.broadcast_to(total, (copies, 1, 128))


def combine(received, first, second, solution_block):
    total = jnp.sum(received[...], axis=0)
    lane = lanes_of((1, 128))
    inner0, curve0, cross, curve_second = [
        jnp.sum(jnp.where(lane == index, total, 0.0), axis=1, keepdims=True) for index in range(4)
    ]
    step0 = inner0 / curve0
    inner1 = inner0 - 2.0 * step0 * curve0 + step0 * step0 * cross
    grow = 1.0 + inner1 / inner0
    curve1 = grow * grow * curve0 - 2.0 * grow * step0 * cross + step0 * step0 * curve_second
    step1 = inner1 / curve1
    solution_block[...] = (step0 + step1 * grow) * first[...] - (step1 * step0) * second[...]


def exchange(last, first, axis):
    count = lax.axis_size(axis)
    forward = [(i, i + 1) for i in range(count - 1)]
    backward = [(target, source) for source, target in forward]
    return lax.ppermute(last, axis, forward), lax.ppermute(first, axis, backward)


def shards(right_side, seam_mask, patch_inverse, row_coupling, col_coupling):
    frame_count, row_count, col_count = (lax.axis_size(axis) for axis in ("tm", "row", "col"))
    peers = row_count * col_count
    coarse_rows = 2 * row_count
    place = jnp.stack([lax.axis_index("row"), lax.axis_index("col")]).astype(jnp.int32)
    block = right_side.reshape(3, ROWS, COLS)
    mask = seam_mask.reshape(ROWS, COLS)
    last, first = call(edges, [(4, RIM, COLS)] * 2, "vv")(block, mask)
    low, high = exchange(last, first, "row")

    mixers = call(
        functools.partial(prepare, row_count, col_count),
        [(coarse_rows, coarse_rows), (SPREAD, coarse_rows), (128, 128), (128, LANES), (PATCHES, 1)],
        "svv",
    )(place, row_coupling, col_coupling)

    tall, to_right, to_left, cells = call(
        assemble, [(4, TALL, LANES), (4, TALL, 128), (4, TALL, 128), (8, 128)], "hhhh"
    )(low, block, mask, high)
    left, right = exchange(to_right, to_left, "col")
    left, right, *mixers = lax.optimization_barrier((left, right, *mixers))
    row_mix, row_spread, col_mix, col_spread, keep = mixers
    work = [
        pltpu.VMEM((PATCHES, 1024), bf16),
        pltpu.VMEM((PATCHES, 1024), bf16),
        pltpu.VMEM((PATCHES, 1024), f32),
        pltpu.VMEM((1024, 1024), bf16),
        pltpu.VMEM((1024, 1024), bf16),
    ]
    flat = pltpu.VMEM((3, FLAT, 128), f32)
    result, screen, share = call(
        functools.partial(first_apply, row_count, col_count),
        [(3, FLAT, 128), (TALL, LANES), (3 * ROWS + 8, LANES)],
        "svvvvvv",
        [flat] + work,
        16,
    )(place, tall, left, right, cells, patch_inverse, keep)
    before, after = exchange(share, share, "tm")
    image, last, first, message = call(
        functools.partial(first_image, peers, row_count, col_count),
        [(3, ROWS, LANES), (3, RIM, LANES), (3, RIM, LANES), (peers, 1, LANES)],
        "svvvvv",
    )(place, result, before, after, screen, cells)
    low, high = exchange(last, first, "row")
    message, low, high = lax.optimization_barrier((message, low, high))
    gathered = lax.all_to_all(message, ("row", "col"), 0, 0)
    first, second, partial = call(
        functools.partial(second_apply, row_count, col_count),
        [(3 * ROWS, COLS), (3 * ROWS, COLS), (1, 128)],
        "s" + "v" * 13,
        [flat] * 2 + work + [pltpu.VMEM((3, SPREAD, LANES), f32)] * 3 + [pltpu.VMEM((3, peers, 128), f32)],
        20,
    )(
        place, gathered, tall, result, image, low, high, screen, patch_inverse, keep,
        row_mix, col_mix, row_spread, col_spread,
    )
    forward = [(i, i + 1) for i in range(frame_count - 1)]
    previous = lax.ppermute(second, "tm", forward)
    (shared,) = call(functools.partial(couple, frame_count), [(frame_count, 1, 128)], "vvv")(second, previous, partial)
    received = lax.all_to_all(shared, "tm", 0, 0)
    (shared,) = call(functools.partial(regroup, peers), [(peers, 1, 128)], "v")(received)
    received = lax.all_to_all(shared, ("row", "col"), 0, 0)
    (answer,) = call(combine, [(3 * ROWS, COLS)], "vvv")(received, first, second)
    return answer.reshape(right_side.shape)


def solution(mesh):
    in_specs = (P(None, "tm", "row", "col"), P("tm", "row", "col"), P(), P(), P())
    out_specs = P(None, "tm", "row", "col")
    return jax.shard_map(shards, mesh=mesh, in_specs=in_specs, out_specs=out_specs, check_vma=False)
```

```python
import functools

import jax
import jax.numpy as jnp
from jax import lax
from jax.experimental import pallas as pl
from jax.experimental.pallas import tpu as pltpu
from jax.sharding import PartitionSpec as P

CELL = 16
RIM = 24
SIDE = 56
seam_screen = 0.1
keep_screen = 2.0
highest = lax.Precision.HIGHEST
f32 = jnp.float32
bf16 = jnp.bfloat16

ROWS = 32
COLS = 256
TALL = ROWS + 2 * RIM
LANES = 384
PATCH_ROWS = 16
PATCH_COLS = 22
PATCHES = PATCH_ROWS * PATCH_COLS
FLAT = 272
SPREAD = 96


def call(body, outs, kinds, scratch=(), limit=8, kept=f32):
    specs = [pl.BlockSpec(memory_space=pltpu.SMEM) if kind == "s" else pl.BlockSpec() for kind in kinds]
    return pl.pallas_call(
        body,
        out_shape=[jax.ShapeDtypeStruct(shape, kept) for shape in outs],
        in_specs=specs,
        scratch_shapes=list(scratch),
        compiler_params=pltpu.CompilerParams(vmem_limit_bytes=limit * 1024 * 1024),
    )


def lanes_of(shape):
    return lax.broadcasted_iota(jnp.int32, shape, len(shape) - 1)


def rows_of(ref, start, count):
    return jnp.concatenate([ref[group, pl.ds(start, count), :] for group in range(3)], axis=1)


def put_rows(ref, start, count, value):
    for group in range(3):
        ref[group, pl.ds(start, count), :] = value[:, 128 * group : 128 * group + 128]


def stripe_of(ref, start):
    return jnp.concatenate([ref.at[group][pl.ds(start, PATCH_ROWS, stride=CELL), :] for group in range(3)], axis=1)


def swap_blocks(parts):
    lane = lanes_of(parts[0].shape)
    for step in (1, 2):
        taken = (lane // (32 * step)) % 2 == 1
        fresh = list(parts)
        for low in range(4):
            if low & step:
                continue
            first, second = parts[low], parts[low + step]
            fresh[low] = jnp.where(taken, pltpu.roll(second, 32 * step, 1), first)
            fresh[low + step] = jnp.where(taken, second, pltpu.roll(first, 128 - 32 * step, 1))
        parts = fresh
    return parts


def patch_apply(span_of, field, result, high_w, low_w, keep, high_x, low_x, solved):
    start, stop = span_of
    used = pl.ds(0, PATCH_ROWS * (stop - start))

    for block in range(8):
        slabs = [stripe_of(field, 4 * block + row) for row in range(4)]
        for parity in range(2):
            if parity:
                slabs = [pltpu.roll(slab, LANES - CELL, 1) for slab in slabs]
            for group in range(3):
                parts = swap_blocks([slab[:, 128 * group : 128 * group + 128] for slab in slabs])
                for inner in range(4):
                    place = 8 * group + 2 * inner + parity
                    if not start <= place < stop:
                        continue
                    upper = parts[inner].astype(bf16)
                    lower = (parts[inner] - upper.astype(f32)).astype(bf16)
                    where = (pl.ds(PATCH_ROWS * (place - start), PATCH_ROWS), pl.ds(128 * block, 128))
                    high_x[where] = upper
                    low_x[where] = lower
    for part in range(4):
        span = pl.ds(256 * part, 256)
        dot = functools.partial(jnp.dot, preferred_element_type=f32)
        total = dot(high_x[used, :], high_w[:, span]) + dot(high_x[used, :], low_w[:, span])
        total = total + dot(low_x[used, :], high_w[:, span])
        solved[used, span] = total * keep[pl.ds(PATCH_ROWS * start, PATCH_ROWS * (stop - start)), :]
    put_rows(result, FLAT - CELL, CELL, jnp.zeros((CELL, LANES), f32))
    for block in range(8):
        sums = None
        for parity in range(2):
            slabs = [[] for _ in range(4)]
            for group in range(3):
                parts = []
                for inner in range(4):
                    place = 8 * group + 2 * inner + parity
                    if not start <= place < stop:
                        parts.append(jnp.zeros((PATCH_ROWS, 128), f32))
                    else:
                        parts.append(solved[pl.ds(PATCH_ROWS * (place - start), PATCH_ROWS), pl.ds(128 * block, 128)])
                for row, piece in enumerate(swap_blocks(parts)):
                    slabs[row].append(piece)
            wide = [jnp.concatenate(pieces, axis=1) for pieces in slabs]
            if parity:
                sums = [total + pltpu.roll(slab, CELL, 1) for total, slab in zip(sums, wide)]
            else:
                sums = wide
        for row in range(4):
            total = sums[row]
            if block >= 4:
                total = total + stripe_of(result, 4 * block + row)
            for group in range(3):
                spot = pl.ds(4 * block + row, PATCH_ROWS, stride=CELL)
                result.at[group][spot, :] = total[:, 128 * group : 128 * group + 128]


def inside_of(place, row_count, col_count, rim):
    row = lax.broadcasted_iota(jnp.int32, (TALL, LANES), 0) + (place[0] * ROWS - RIM)
    lane = lanes_of((TALL, LANES))
    col = lane + (place[1] * COLS - SIDE)
    near = (lane >= SIDE - rim) & (lane < SIDE + COLS + rim)
    return (row >= 0) & (row < ROWS * row_count) & (col >= 0) & (col < COLS * col_count) & near


def fold_rows(edge):
    half = TALL // 2
    lane = lanes_of((half, 128))
    return jnp.where(lane < 64, edge[:half], pltpu.roll(edge[half:], 64, 1))


def merge_sides(middle, left, right):
    left = jnp.concatenate([left, pltpu.roll(left, 64, 1)], axis=0)
    right = jnp.concatenate([pltpu.roll(right, SIDE, 1), pltpu.roll(right, SIDE + 64, 1)], axis=0)
    lane = lanes_of(left.shape)
    first = jnp.where(lane < SIDE, left, middle[:, :128])
    last = jnp.where((lane >= SIDE) & (lane < 2 * SIDE), right, middle[:, 256:])
    return jnp.concatenate([first, middle[:, 128:256], last], axis=1)


def cell_sums(blocks):
    rows = [jnp.sum(block[CELL * half : CELL * half + CELL], axis=0, keepdims=True) for block in blocks for half in range(2)]
    lane = lax.broadcasted_iota(jnp.int32, (LANES, 128), 0) - SIDE
    cell = lanes_of((LANES, 128))
    inside = (lane >= CELL * cell) & (lane < CELL * cell + CELL) & (cell < COLS // CELL)
    stacked = jnp.concatenate(rows, axis=0)
    return jnp.dot(stacked, inside.astype(f32), precision=highest, preferred_element_type=f32)


def assemble(low, middle, high, tall, to_right, to_left, cells):
    own = []
    for channel in range(4):
        column = jnp.concatenate([low[channel], middle[channel], high[channel]], axis=0)
        wide = jnp.concatenate([column, jnp.zeros((TALL, 128), f32)], axis=1)
        wide = pltpu.roll(wide, SIDE, 1)
        tall[channel] = wide
        to_right[channel] = fold_rows(wide[:, 256:])
        to_left[channel] = fold_rows(pltpu.roll(wide[:, :128], 128 - SIDE, 1))
        own.append(wide[RIM : RIM + ROWS])
    cells[...] = cell_sums(own)


def prepare(row_count, col_count, place, row_coupling, col_coupling, row_mix, row_spread, col_mix, col_spread):
    dot = functools.partial(jnp.dot, precision=highest, preferred_element_type=f32)
    turned = functools.partial(
        lax.dot_general, dimension_numbers=(((1,), (1,)), ((), ())), precision=highest, preferred_element_type=f32
    )
    coarse_rows, coarse_cols = 2 * row_count, CELL * col_count

    def matrix(shape, rule):
        return rule(lax.broadcasted_iota(jnp.int32, shape, 0), lanes_of(shape)).astype(f32)

    order = matrix((coarse_rows, coarse_rows), lambda i, j: (j // 2 == i % row_count) & (j % 2 == i // row_count))
    swapped = turned(row_coupling[...], order)
    row_mix[...] = dot(order, swapped)
    row_pick = matrix((SPREAD, coarse_rows), lambda i, j: (i + place[0] * ROWS - ROWS + CELL * 2) // CELL - 2 == j)
    row_spread[...] = dot(row_pick, swapped)
    col_turned = turned(matrix((128, coarse_cols), lambda i, j: i == j), col_coupling[...])
    col_mix[...] = dot(col_turned, matrix((coarse_cols, 128), lambda i, j: i == j))

    def column(cell, lane):
        col = lane + (place[1] * COLS - SIDE)
        return (col >= CELL * cell) & (col < CELL * cell + CELL)

    col_spread[...] = dot(col_turned, matrix((coarse_cols, LANES), column))


def split(whole, upper, lower):
    for part in range(16):
        span = pl.ds(64 * part, 64)
        high = whole[span, :].astype(bf16)
        upper[span, :] = high
        lower[span, :] = (whole[span, :] - high.astype(f32)).astype(bf16)


def edges(block, mask, last, first, middle):
    for channel in range(3):
        middle[channel] = block[channel]
        last[channel] = block[channel, ROWS - RIM :]
        first[channel] = block[channel, :RIM]
    screen = jnp.where(mask[...] == 1, seam_screen, keep_screen).astype(f32)
    middle[3] = screen
    last[3] = screen[ROWS - RIM :]
    first[3] = screen[:RIM]


def first_apply(
    row_count, col_count, place, tall, left, right, cells, high_w, low_w, keep, result, screen, share,
    field, high_x, low_x, solved,
):
    put_rows(field, 240, FLAT - 240, jnp.zeros((FLAT - 240, LANES), f32))
    for channel in range(3):
        put_rows(field, TALL * channel, TALL, merge_sides(tall[channel], left[channel], right[channel]))
    screen[...] = merge_sides(tall[3], left[3], right[3])
    patch_apply((0, PATCH_COLS), field, result, high_w, low_w, keep, high_x, low_x, solved)
    inside = inside_of(place, row_count, col_count, 40)
    for channel in range(3):
        whole = rows_of(result, TALL * channel, TALL)
        put_rows(result, TALL * channel, TALL, jnp.where(inside, whole, 0.0))
        share[pl.ds(ROWS * channel, ROWS), :] = rows_of(result, TALL * channel + RIM, ROWS)
    share[pl.ds(3 * ROWS, 8), :] = jnp.concatenate([cells[...], jnp.zeros((8, 256), f32)], axis=1)


def first_image(copies, row_count, col_count, place, result, before, after, screen, cells, image, last, first, message):
    inside = inside_of(place, row_count, col_count, RIM)[RIM : RIM + ROWS]
    blocks = []
    for channel in range(3):
        base = TALL * channel + RIM
        center = rows_of(result, base, ROWS)
        near = rows_of(result, base - 1, ROWS) + rows_of(result, base + 1, ROWS)
        near = near + pltpu.roll(center, 1, 1) + pltpu.roll(center, LANES - 1, 1)
        span = pl.ds(ROWS * channel, ROWS)
        value = (screen[pl.ds(RIM, ROWS), :] + 6.0) * center - near - before[span, :] - after[span, :]
        value = jnp.where(inside, value, 0.0)
        image[channel] = value
        last[channel] = value[ROWS - RIM :]
        first[channel] = value[:RIM]
        blocks.append(value)
    sums = cell_sums(blocks)
    beside = before[pl.ds(3 * ROWS, 8), :128] + after[pl.ds(3 * ROWS, 8), :128]
    rows = [cells[0:6], beside[0:6], sums, cells[6:8]]
    rows = [part[row : row + 1] for part in rows for row in range(part.shape[0])]
    lane = lanes_of((1, 128))
    packed = []
    for group in range(3):
        total = jnp.zeros((1, 128), f32)
        for spot in range(8):
            if 8 * group + spot < len(rows):
                row = rows[8 * group + spot]
                row = pltpu.roll(row, CELL * spot, 1) if spot else row
                total = jnp.where(lane // CELL == spot, row, total)
        packed.append(total)
    message[...] = jnp.broadcast_to(jnp.concatenate(packed, axis=1)[None], (copies, 1, LANES))


def second_apply(
    row_count, col_count, place, gathered, block, result, image, low, high, screen, inverse,
    keep, row_mix, col_mix, row_spread, col_spread, first, second, partial,
    field, output, high_x, low_x, solved, high_w, low_w, coarse, beside, late, letters,
):
    dot = functools.partial(jnp.dot, precision=highest, preferred_element_type=f32)
    coarse_rows = 2 * row_count
    lane = lanes_of((row_count, 128))
    for group in range(3):
        letters[group] = gathered[:, 0, 128 * group : 128 * group + 128]

    def grid_of(index):
        halves = []
        for half in range(2):
            chunk = 2 * index + half
            total = jnp.zeros((row_count, 128), f32)
            for col in range(col_count):
                piece = letters.at[chunk // 8][pl.ds(col, row_count, stride=col_count), :]
                shift = (CELL * col - CELL * (chunk % 8)) % 128
                piece = pltpu.roll(piece, shift, 1) if shift else piece
                total = jnp.where(lane // CELL == col, piece, total)
            halves.append(total)
        return jnp.concatenate(halves, axis=0)

    def beside_each_other(tall, width):
        count = tall.shape[0] // coarse_rows
        return jnp.concatenate([tall[coarse_rows * i : coarse_rows * (i + 1)] for i in range(count)], axis=1)

    def spread(tall, targets):
        wide = dot(row_spread[...], beside_each_other(dot(tall, col_spread[...]), LANES))
        for index, (ref, channel) in enumerate(targets):
            ref[channel] = wide[:, LANES * index : LANES * (index + 1)]

    screen_cells = grid_of(9)
    grid_lane = lanes_of((coarse_rows, 128))
    zero_row = jnp.zeros((1, 128), f32)
    inside = inside_of(place, row_count, col_count, RIM)
    tall_lane = lanes_of((ROWS, LANES))
    own = (tall_lane >= SIDE) & (tall_lane < SIDE + COLS)
    put_rows(field, 240, FLAT - 240, jnp.zeros((FLAT - 240, LANES), f32))
    sums = jnp.concatenate([grid_of(index) for index in range(6)], axis=0)
    spread(sums, [(coarse, 0), (coarse, 1), (coarse, 2), (beside, 0), (beside, 1), (beside, 2)])
    for channel in range(3):
        center = coarse[channel, pl.ds(8, TALL), :]
        near = coarse[channel, pl.ds(7, TALL), :] + coarse[channel, pl.ds(9, TALL), :]
        near = near + pltpu.roll(center, 1, 1) + pltpu.roll(center, LANES - 1, 1)
        value = (screen[...] + 6.0) * center - near - beside[channel, pl.ds(8, TALL), :]
        middle = jnp.concatenate([low[channel], image[channel], high[channel]], axis=0)
        value = value + middle
        put_rows(field, TALL * channel, TALL, jnp.where(inside, value, 0.0))
    levels = dot(row_mix[...], beside_each_other(dot(sums, col_mix[...]), 128))
    late_sums = []
    for channel in range(3):
        level = levels[:, 128 * channel : 128 * channel + 128]
        level_beside = levels[:, 384 + 128 * channel : 512 + 128 * channel]
        even, odd = level[:row_count], level[row_count:]
        above = jnp.concatenate([zero_row, odd[:-1], even], axis=0)
        below = jnp.concatenate([odd, even[1:], zero_row], axis=0)
        before = jnp.where(grid_lane == 0, 0.0, pltpu.roll(level, 1, 1))
        after = jnp.where(grid_lane == CELL * col_count - 1, 0.0, pltpu.roll(level, 127, 1))
        image_sums = grid_of(6 + channel) + (screen_cells + 576.0) * level
        late_sums.append(image_sums - 16.0 * (above + below + before + after) - 256.0 * level_beside)
    spread(jnp.concatenate(late_sums, axis=0), [(late, 0), (late, 1), (late, 2)])
    split(inverse, high_w, low_w)
    patch_apply((2, PATCH_COLS - 2), field, output, high_w, low_w, keep, high_x, low_x, solved)
    totals = [jnp.zeros((ROWS, LANES), f32) for _ in range(4)]
    for channel in range(3):
        whole = rows_of(output, TALL * channel, TALL) + late[channel, pl.ds(8, TALL), :]
        put_rows(output, TALL * channel, TALL, jnp.where(inside, whole, 0.0))
        base = TALL * channel + RIM
        new = rows_of(output, base, ROWS)
        near = rows_of(output, base - 1, ROWS) + rows_of(output, base + 1, ROWS)
        near = near + pltpu.roll(new, 1, 1) + pltpu.roll(new, LANES - 1, 1)
        new_image = (screen[pl.ds(RIM, ROWS), :] + 6.0) * new - near
        old = jnp.where(own, rows_of(result, base, ROWS) + coarse[channel, pl.ds(8 + RIM, ROWS), :], 0.0)
        new = jnp.where(own, new, 0.0)
        old_image = jnp.where(own, rows_of(field, base, ROWS), 0.0)
        totals[0] = totals[0] + block[channel, pl.ds(RIM, ROWS), :] * old
        totals[1] = totals[1] + old * old_image
        totals[2] = totals[2] + old_image * new
        totals[3] = totals[3] + new * new_image
        first[pl.ds(ROWS * channel, ROWS), :] = pltpu.roll(old, LANES - SIDE, 1)[:, :COLS]
        second[pl.ds(ROWS * channel, ROWS), :] = pltpu.roll(new, LANES - SIDE, 1)[:, :COLS]
    lane = lanes_of((1, 128))
    packed = jnp.zeros((1, 128), f32)
    for index, total in enumerate(totals):
        value = jnp.sum(jnp.sum(total, axis=0, keepdims=True), axis=1, keepdims=True)
        packed = jnp.where(lane == index, value, packed)
    partial[...] = packed


def couple(copies, second, before, partial, shared):
    product = second[...] * before[...]
    value = jnp.sum(jnp.sum(product, axis=0, keepdims=True), axis=1, keepdims=True)
    packed = partial[...] - jnp.where(lanes_of((1, 128)) == 3, 2.0 * value, 0.0)
    shared[...] = jnp.broadcast_to(packed[None], (copies, 1, 128))


def regroup(copies, received, shared):
    total = jnp.sum(received[...], axis=0, keepdims=True)
    shared[...] = jnp.broadcast_to(total, (copies, 1, 128))


def combine(received, first, second, solution_block):
    total = jnp.sum(received[...], axis=0)
    lane = lanes_of((1, 128))
    inner0, curve0, cross, curve_second = [
        jnp.sum(jnp.where(lane == index, total, 0.0), axis=1, keepdims=True) for index in range(4)
    ]
    step0 = inner0 / curve0
    inner1 = inner0 - 2.0 * step0 * curve0 + step0 * step0 * cross
    grow = 1.0 + inner1 / inner0
    curve1 = grow * grow * curve0 - 2.0 * grow * step0 * cross + step0 * step0 * curve_second
    step1 = inner1 / curve1
    solution_block[...] = (step0 + step1 * grow) * first[...] - (step1 * step0) * second[...]


def exchange(last, first, axis):
    count = lax.axis_size(axis)
    forward = [(i, i + 1) for i in range(count - 1)]
    backward = [(target, source) for source, target in forward]
    return lax.ppermute(last, axis, forward), lax.ppermute(first, axis, backward)


def shards(right_side, seam_mask, patch_inverse, row_coupling, col_coupling):
    frame_count, row_count, col_count = (lax.axis_size(axis) for axis in ("tm", "row", "col"))
    peers = row_count * col_count
    coarse_rows = 2 * row_count
    place = jnp.stack([lax.axis_index("row"), lax.axis_index("col")]).astype(jnp.int32)
    block = right_side.reshape(3, ROWS, COLS)
    mask = seam_mask.reshape(ROWS, COLS)
    last, first, middle = call(edges, [(4, RIM, COLS)] * 2 + [(4, ROWS, COLS)], "vv")(block, mask)
    low, high = exchange(last, first, "row")

    index = lax.broadcasted_iota(jnp.int32, (PATCHES, 1), 0)
    kind = index % PATCH_ROWS
    patch_row = 2 * place[0] + kind % 5 - 1
    patch_col = CELL * place[1] + index // PATCH_ROWS - 3
    kept = (kind < 15) & (kind % 5 < 4) & (patch_row >= 0) & (patch_row < coarse_rows)
    keep = (kept & (patch_col >= 0) & (patch_col < CELL * col_count)).astype(f32)

    tall, to_right, to_left, cells = call(
        assemble, [(4, TALL, LANES), (4, TALL // 2, 128), (4, TALL // 2, 128), (8, 128)], "vvv"
    )(low, middle, high)
    to_right, to_left, whole = lax.optimization_barrier((to_right, to_left, patch_inverse))
    left, right = exchange(to_right, to_left, "col")
    high_w, low_w = call(split, [(1024, 1024)] * 2, "v", limit=16, kept=bf16)(whole)
    left, right, high_w, low_w = lax.optimization_barrier((left, right, high_w, low_w))
    work = [
        pltpu.VMEM((PATCHES, 1024), bf16),
        pltpu.VMEM((PATCHES, 1024), bf16),
        pltpu.VMEM((PATCHES, 1024), f32),
    ]
    flat = pltpu.VMEM((3, FLAT, 128), f32)
    result, screen, share = call(
        functools.partial(first_apply, row_count, col_count),
        [(3, FLAT, 128), (TALL, LANES), (3 * ROWS + 8, LANES)],
        "svvvvvvv",
        [flat] + work,
        16,
    )(place, tall, left, right, cells, high_w, low_w, keep)
    before, after = exchange(share, share, "tm")
    image, last, first, message = call(
        functools.partial(first_image, peers, row_count, col_count),
        [(3, ROWS, LANES), (3, RIM, LANES), (3, RIM, LANES), (peers, 1, LANES)],
        "svvvvv",
    )(place, result, before, after, screen, cells)
    low, high = exchange(last, first, "row")
    message, row_coupling, col_coupling = lax.optimization_barrier((message, row_coupling, col_coupling))
    row_mix, row_spread, col_mix, col_spread = call(
        functools.partial(prepare, row_count, col_count),
        [(coarse_rows, coarse_rows), (SPREAD, coarse_rows), (128, 128), (128, LANES)],
        "svv",
    )(place, row_coupling, col_coupling)
    gathered = lax.all_to_all(message, ("row", "col"), 0, 0)
    first, second, partial = call(
        functools.partial(second_apply, row_count, col_count),
        [(3 * ROWS, COLS), (3 * ROWS, COLS), (1, 128)],
        "s" + "v" * 13,
        [flat] * 2 + work + [pltpu.VMEM((1024, 1024), bf16)] * 2 + [pltpu.VMEM((3, SPREAD, LANES), f32)] * 3 + [pltpu.VMEM((3, peers, 128), f32)],
        20,
    )(
        place, gathered, tall, result, image, low, high, screen, patch_inverse, keep,
        row_mix, col_mix, row_spread, col_spread,
    )
    forward = [(i, i + 1) for i in range(frame_count - 1)]
    previous = lax.ppermute(second, "tm", forward)
    (shared,) = call(functools.partial(couple, frame_count), [(frame_count, 1, 128)], "vvv")(second, previous, partial)
    received = lax.all_to_all(shared, "tm", 0, 0)
    (shared,) = call(functools.partial(regroup, peers), [(peers, 1, 128)], "v")(received)
    received = lax.all_to_all(shared, ("row", "col"), 0, 0)
    (answer,) = call(combine, [(3 * ROWS, COLS)], "vvv")(received, first, second)
    return answer.reshape(right_side.shape)


def solution(mesh):
    in_specs = (P(None, "tm", "row", "col"), P("tm", "row", "col"), P(), P(), P())
    out_specs = P(None, "tm", "row", "col")
    return jax.shard_map(shards, mesh=mesh, in_specs=in_specs, out_specs=out_specs, check_vma=False)
```

```python
import functools

import jax
import jax.numpy as jnp
from jax import lax
from jax.experimental import pallas as pl
from jax.experimental.pallas import tpu as pltpu
from jax.sharding import PartitionSpec as P

CELL = 16
RIM = 24
SIDE = 56
seam_screen = 0.1
keep_screen = 2.0
highest = lax.Precision.HIGHEST
f32 = jnp.float32
bf16 = jnp.bfloat16

ROWS = 32
COLS = 256
TALL = ROWS + 2 * RIM
LANES = 384
PATCH_ROWS = 16
PATCH_COLS = 22
PATCHES = PATCH_ROWS * PATCH_COLS
FLAT = 272
SPREAD = 96


def call(body, outs, kinds, scratch=(), limit=8, kept=f32):
    specs = [pl.BlockSpec(memory_space=pltpu.SMEM) if kind == "s" else pl.BlockSpec() for kind in kinds]
    return pl.pallas_call(
        body,
        out_shape=[jax.ShapeDtypeStruct(shape, kept) for shape in outs],
        in_specs=specs,
        scratch_shapes=list(scratch),
        compiler_params=pltpu.CompilerParams(vmem_limit_bytes=limit * 1024 * 1024),
    )


def lanes_of(shape):
    return lax.broadcasted_iota(jnp.int32, shape, len(shape) - 1)


def rows_of(ref, start, count):
    return jnp.concatenate([ref[group, pl.ds(start, count), :] for group in range(3)], axis=1)


def put_rows(ref, start, count, value):
    for group in range(3):
        ref[group, pl.ds(start, count), :] = value[:, 128 * group : 128 * group + 128]


def stripe_of(ref, start):
    return jnp.concatenate([ref.at[group][pl.ds(start, PATCH_ROWS, stride=CELL), :] for group in range(3)], axis=1)


def swap_blocks(parts):
    lane = lanes_of(parts[0].shape)
    for step in (1, 2):
        taken = (lane // (32 * step)) % 2 == 1
        fresh = list(parts)
        for low in range(4):
            if low & step:
                continue
            first, second = parts[low], parts[low + step]
            fresh[low] = jnp.where(taken, pltpu.roll(second, 32 * step, 1), first)
            fresh[low + step] = jnp.where(taken, second, pltpu.roll(first, 128 - 32 * step, 1))
        parts = fresh
    return parts


def patch_apply(span_of, field, result, high_w, low_w, keep, high_x, low_x, solved):
    start, stop = span_of
    used = pl.ds(0, PATCH_ROWS * (stop - start))

    for block in range(8):
        slabs = [stripe_of(field, 4 * block + row) for row in range(4)]
        for parity in range(2):
            if parity:
                slabs = [pltpu.roll(slab, LANES - CELL, 1) for slab in slabs]
            for group in range(3):
                parts = swap_blocks([slab[:, 128 * group : 128 * group + 128] for slab in slabs])
                for inner in range(4):
                    place = 8 * group + 2 * inner + parity
                    if not start <= place < stop:
                        continue
                    upper = parts[inner].astype(bf16)
                    lower = (parts[inner] - upper.astype(f32)).astype(bf16)
                    where = (pl.ds(PATCH_ROWS * (place - start), PATCH_ROWS), pl.ds(128 * block, 128))
                    high_x[where] = upper
                    low_x[where] = lower
    for part in range(4):
        span = pl.ds(256 * part, 256)
        dot = functools.partial(jnp.dot, preferred_element_type=f32)
        total = dot(high_x[used, :], high_w[:, span]) + dot(high_x[used, :], low_w[:, span])
        total = total + dot(low_x[used, :], high_w[:, span])
        solved[used, span] = total * keep[pl.ds(PATCH_ROWS * start, PATCH_ROWS * (stop - start)), :]
    put_rows(result, FLAT - CELL, CELL, jnp.zeros((CELL, LANES), f32))
    for block in range(8):
        sums = None
        for parity in range(2):
            slabs = [[] for _ in range(4)]
            for group in range(3):
                parts = []
                for inner in range(4):
                    place = 8 * group + 2 * inner + parity
                    if not start <= place < stop:
                        parts.append(jnp.zeros((PATCH_ROWS, 128), f32))
                    else:
                        parts.append(solved[pl.ds(PATCH_ROWS * (place - start), PATCH_ROWS), pl.ds(128 * block, 128)])
                for row, piece in enumerate(swap_blocks(parts)):
                    slabs[row].append(piece)
            wide = [jnp.concatenate(pieces, axis=1) for pieces in slabs]
            if parity:
                sums = [total + pltpu.roll(slab, CELL, 1) for total, slab in zip(sums, wide)]
            else:
                sums = wide
        for row in range(4):
            total = sums[row]
            if block >= 4:
                total = total + stripe_of(result, 4 * block + row)
            for group in range(3):
                spot = pl.ds(4 * block + row, PATCH_ROWS, stride=CELL)
                result.at[group][spot, :] = total[:, 128 * group : 128 * group + 128]


def inside_of(place, row_count, col_count, rim):
    row = lax.broadcasted_iota(jnp.int32, (TALL, LANES), 0) + (place[0] * ROWS - RIM)
    lane = lanes_of((TALL, LANES))
    col = lane + (place[1] * COLS - SIDE)
    near = (lane >= SIDE - rim) & (lane < SIDE + COLS + rim)
    return (row >= 0) & (row < ROWS * row_count) & (col >= 0) & (col < COLS * col_count) & near


def fold_rows(edge):
    half = TALL // 2
    lane = lanes_of((half, 128))
    return jnp.where(lane < 64, edge[:half], pltpu.roll(edge[half:], 64, 1))


def merge_sides(middle, left, right):
    left = jnp.concatenate([left, pltpu.roll(left, 64, 1)], axis=0)
    right = jnp.concatenate([pltpu.roll(right, SIDE, 1), pltpu.roll(right, SIDE + 64, 1)], axis=0)
    lane = lanes_of(left.shape)
    first = jnp.where(lane < SIDE, left, middle[:, :128])
    last = jnp.where((lane >= SIDE) & (lane < 2 * SIDE), right, middle[:, 256:])
    return jnp.concatenate([first, middle[:, 128:256], last], axis=1)


def cell_sums(blocks):
    rows = [jnp.sum(block[CELL * half : CELL * half + CELL], axis=0, keepdims=True) for block in blocks for half in range(2)]
    lane = lax.broadcasted_iota(jnp.int32, (LANES, 128), 0) - SIDE
    cell = lanes_of((LANES, 128))
    inside = (lane >= CELL * cell) & (lane < CELL * cell + CELL) & (cell < COLS // CELL)
    stacked = jnp.concatenate(rows, axis=0)
    return jnp.dot(stacked, inside.astype(f32), precision=highest, preferred_element_type=f32)


def assemble(low, middle, high, tall, to_right, to_left, cells):
    own = []
    for channel in range(4):
        column = jnp.concatenate([low[channel], middle[channel], high[channel]], axis=0)
        wide = jnp.concatenate([column, jnp.zeros((TALL, 128), f32)], axis=1)
        wide = pltpu.roll(wide, SIDE, 1)
        tall[channel] = wide
        to_right[channel] = fold_rows(wide[:, 256:])
        to_left[channel] = fold_rows(pltpu.roll(wide[:, :128], 128 - SIDE, 1))
        own.append(wide[RIM : RIM + ROWS])
    cells[...] = cell_sums(own)


def prepare(row_count, col_count, place, row_coupling, col_coupling, row_mix, row_spread, col_mix, col_spread):
    dot = functools.partial(jnp.dot, precision=highest, preferred_element_type=f32)
    turned = functools.partial(
        lax.dot_general, dimension_numbers=(((1,), (1,)), ((), ())), precision=highest, preferred_element_type=f32
    )
    coarse_rows, coarse_cols = 2 * row_count, CELL * col_count

    def matrix(shape, rule):
        return rule(lax.broadcasted_iota(jnp.int32, shape, 0), lanes_of(shape)).astype(f32)

    order = matrix((coarse_rows, coarse_rows), lambda i, j: (j // 2 == i % row_count) & (j % 2 == i // row_count))
    swapped = turned(row_coupling[...], order)
    row_mix[...] = dot(order, swapped)
    row_pick = matrix((SPREAD, coarse_rows), lambda i, j: (i + place[0] * ROWS - ROWS + CELL * 2) // CELL - 2 == j)
    row_spread[...] = dot(row_pick, swapped)
    col_turned = turned(matrix((128, coarse_cols), lambda i, j: i == j), col_coupling[...])
    col_mix[...] = dot(col_turned, matrix((coarse_cols, 128), lambda i, j: i == j))

    def column(cell, lane):
        col = lane + (place[1] * COLS - SIDE)
        return (col >= CELL * cell) & (col < CELL * cell + CELL)

    col_spread[...] = dot(col_turned, matrix((coarse_cols, LANES), column))


def split(whole, upper, lower):
    for part in range(16):
        span = pl.ds(64 * part, 64)
        high = whole[span, :].astype(bf16)
        upper[span, :] = high
        lower[span, :] = (whole[span, :] - high.astype(f32)).astype(bf16)


def edges(block, mask, last, first, middle):
    for channel in range(3):
        middle[channel] = block[channel]
        last[channel] = block[channel, ROWS - RIM :]
        first[channel] = block[channel, :RIM]
    screen = jnp.where(mask[...] == 1, seam_screen, keep_screen).astype(f32)
    middle[3] = screen
    last[3] = screen[ROWS - RIM :]
    first[3] = screen[:RIM]


def first_apply(
    row_count, col_count, place, tall, left, right, cells, high_w, low_w, keep, result, screen, share,
    field, high_x, low_x, solved,
):
    put_rows(field, 240, FLAT - 240, jnp.zeros((FLAT - 240, LANES), f32))
    for channel in range(3):
        put_rows(field, TALL * channel, TALL, merge_sides(tall[channel], left[channel], right[channel]))
    screen[...] = merge_sides(tall[3], left[3], right[3])
    patch_apply((0, PATCH_COLS), field, result, high_w, low_w, keep, high_x, low_x, solved)
    inside = inside_of(place, row_count, col_count, 40)
    for channel in range(3):
        whole = rows_of(result, TALL * channel, TALL)
        put_rows(result, TALL * channel, TALL, jnp.where(inside, whole, 0.0))
        share[pl.ds(ROWS * channel, ROWS), :] = rows_of(result, TALL * channel + RIM, ROWS)
    share[pl.ds(3 * ROWS, 8), :] = jnp.concatenate([cells[...], jnp.zeros((8, 256), f32)], axis=1)


def first_image(copies, row_count, col_count, place, result, before, after, screen, cells, image, last, first, message):
    inside = inside_of(place, row_count, col_count, RIM)[RIM : RIM + ROWS]
    blocks = []
    for channel in range(3):
        base = TALL * channel + RIM
        center = rows_of(result, base, ROWS)
        near = rows_of(result, base - 1, ROWS) + rows_of(result, base + 1, ROWS)
        near = near + pltpu.roll(center, 1, 1) + pltpu.roll(center, LANES - 1, 1)
        span = pl.ds(ROWS * channel, ROWS)
        value = (screen[pl.ds(RIM, ROWS), :] + 6.0) * center - near - before[span, :] - after[span, :]
        value = jnp.where(inside, value, 0.0)
        image[channel] = value
        last[channel] = value[ROWS - RIM :]
        first[channel] = value[:RIM]
        blocks.append(value)
    sums = cell_sums(blocks)
    beside = before[pl.ds(3 * ROWS, 8), :128] + after[pl.ds(3 * ROWS, 8), :128]
    rows = [cells[0:6], beside[0:6], sums, cells[6:8]]
    rows = [part[row : row + 1] for part in rows for row in range(part.shape[0])]
    lane = lanes_of((1, 128))
    packed = []
    for group in range(3):
        total = jnp.zeros((1, 128), f32)
        for spot in range(8):
            if 8 * group + spot < len(rows):
                row = rows[8 * group + spot]
                row = pltpu.roll(row, CELL * spot, 1) if spot else row
                total = jnp.where(lane // CELL == spot, row, total)
        packed.append(total)
    message[...] = jnp.broadcast_to(jnp.concatenate(packed, axis=1)[None], (copies, 1, LANES))


def second_apply(
    row_count, col_count, place, gathered, block, result, image, low, high, screen, inverse,
    keep, row_mix, col_mix, row_spread, col_spread, first, second, partial,
    field, output, high_x, low_x, solved, high_w, low_w, coarse, beside, late, letters,
):
    dot = functools.partial(jnp.dot, precision=highest, preferred_element_type=f32)
    coarse_rows = 2 * row_count
    lane = lanes_of((row_count, 128))
    for group in range(3):
        letters[group] = gathered[:, 0, 128 * group : 128 * group + 128]

    def grid_of(index):
        halves = []
        for half in range(2):
            chunk = 2 * index + half
            total = jnp.zeros((row_count, 128), f32)
            for col in range(col_count):
                piece = letters.at[chunk // 8][pl.ds(col, row_count, stride=col_count), :]
                shift = (CELL * col - CELL * (chunk % 8)) % 128
                piece = pltpu.roll(piece, shift, 1) if shift else piece
                total = jnp.where(lane // CELL == col, piece, total)
            halves.append(total)
        return jnp.concatenate(halves, axis=0)

    def beside_each_other(tall, width):
        count = tall.shape[0] // coarse_rows
        return jnp.concatenate([tall[coarse_rows * i : coarse_rows * (i + 1)] for i in range(count)], axis=1)

    def spread(tall, targets):
        wide = dot(row_spread[...], beside_each_other(dot(tall, col_spread[...]), LANES))
        for index, (ref, channel) in enumerate(targets):
            ref[channel] = wide[:, LANES * index : LANES * (index + 1)]

    screen_cells = grid_of(9)
    grid_lane = lanes_of((coarse_rows, 128))
    zero_row = jnp.zeros((1, 128), f32)
    inside = inside_of(place, row_count, col_count, RIM)
    tall_lane = lanes_of((ROWS, LANES))
    own = (tall_lane >= SIDE) & (tall_lane < SIDE + COLS)
    put_rows(field, 240, FLAT - 240, jnp.zeros((FLAT - 240, LANES), f32))
    sums = jnp.concatenate([grid_of(index) for index in range(6)], axis=0)
    spread(sums, [(coarse, 0), (coarse, 1), (coarse, 2), (beside, 0), (beside, 1), (beside, 2)])
    for channel in range(3):
        center = coarse[channel, pl.ds(8, TALL), :]
        near = coarse[channel, pl.ds(7, TALL), :] + coarse[channel, pl.ds(9, TALL), :]
        near = near + pltpu.roll(center, 1, 1) + pltpu.roll(center, LANES - 1, 1)
        value = (screen[...] + 6.0) * center - near - beside[channel, pl.ds(8, TALL), :]
        middle = jnp.concatenate([low[channel], image[channel], high[channel]], axis=0)
        value = value + middle
        put_rows(field, TALL * channel, TALL, jnp.where(inside, value, 0.0))
    levels = dot(row_mix[...], beside_each_other(dot(sums, col_mix[...]), 128))
    late_sums = []
    for channel in range(3):
        level = levels[:, 128 * channel : 128 * channel + 128]
        level_beside = levels[:, 384 + 128 * channel : 512 + 128 * channel]
        even, odd = level[:row_count], level[row_count:]
        above = jnp.concatenate([zero_row, odd[:-1], even], axis=0)
        below = jnp.concatenate([odd, even[1:], zero_row], axis=0)
        before = jnp.where(grid_lane == 0, 0.0, pltpu.roll(level, 1, 1))
        after = jnp.where(grid_lane == CELL * col_count - 1, 0.0, pltpu.roll(level, 127, 1))
        image_sums = grid_of(6 + channel) + (screen_cells + 576.0) * level
        late_sums.append(image_sums - 16.0 * (above + below + before + after) - 256.0 * level_beside)
    spread(jnp.concatenate(late_sums, axis=0), [(late, 0), (late, 1), (late, 2)])
    split(inverse, high_w, low_w)
    patch_apply((2, PATCH_COLS - 2), field, output, high_w, low_w, keep, high_x, low_x, solved)
    totals = [jnp.zeros((ROWS, LANES), f32) for _ in range(4)]
    for channel in range(3):
        whole = rows_of(output, TALL * channel, TALL) + late[channel, pl.ds(8, TALL), :]
        put_rows(output, TALL * channel, TALL, jnp.where(inside, whole, 0.0))
        base = TALL * channel + RIM
        new = rows_of(output, base, ROWS)
        near = rows_of(output, base - 1, ROWS) + rows_of(output, base + 1, ROWS)
        near = near + pltpu.roll(new, 1, 1) + pltpu.roll(new, LANES - 1, 1)
        new_image = (screen[pl.ds(RIM, ROWS), :] + 6.0) * new - near
        old = jnp.where(own, rows_of(result, base, ROWS) + coarse[channel, pl.ds(8 + RIM, ROWS), :], 0.0)
        new = jnp.where(own, new, 0.0)
        old_image = jnp.where(own, rows_of(field, base, ROWS), 0.0)
        totals[0] = totals[0] + block[channel, pl.ds(RIM, ROWS), :] * old
        totals[1] = totals[1] + old * old_image
        totals[2] = totals[2] + old_image * new
        totals[3] = totals[3] + new * new_image
        first[pl.ds(ROWS * channel, ROWS), :] = pltpu.roll(old, LANES - SIDE, 1)[:, :COLS]
        second[pl.ds(ROWS * channel, ROWS), :] = pltpu.roll(new, LANES - SIDE, 1)[:, :COLS]
    lane = lanes_of((1, 128))
    packed = jnp.zeros((1, 128), f32)
    for index, total in enumerate(totals):
        value = jnp.sum(jnp.sum(total, axis=0, keepdims=True), axis=1, keepdims=True)
        packed = jnp.where(lane == index, value, packed)
    partial[...] = packed


def couple(copies, second, before, partial, shared):
    product = second[...] * before[...]
    value = jnp.sum(jnp.sum(product, axis=0, keepdims=True), axis=1, keepdims=True)
    packed = partial[...] - jnp.where(lanes_of((1, 128)) == 3, 2.0 * value, 0.0)
    shared[...] = jnp.broadcast_to(packed[None], (copies, 1, 128))


def regroup(copies, received, shared):
    total = jnp.sum(received[...], axis=0, keepdims=True)
    shared[...] = jnp.broadcast_to(total, (copies, 1, 128))


def combine(received, first, second, solution_block):
    total = jnp.sum(received[...], axis=0)
    lane = lanes_of((1, 128))
    inner0, curve0, cross, curve_second = [
        jnp.sum(jnp.where(lane == index, total, 0.0), axis=1, keepdims=True) for index in range(4)
    ]
    step0 = inner0 / curve0
    inner1 = inner0 - 2.0 * step0 * curve0 + step0 * step0 * cross
    grow = 1.0 + inner1 / inner0
    curve1 = grow * grow * curve0 - 2.0 * grow * step0 * cross + step0 * step0 * curve_second
    step1 = inner1 / curve1
    solution_block[...] = (step0 + step1 * grow) * first[...] - (step1 * step0) * second[...]


def exchange(last, first, axis):
    count = lax.axis_size(axis)
    forward = [(i, i + 1) for i in range(count - 1)]
    backward = [(target, source) for source, target in forward]
    return lax.ppermute(last, axis, forward), lax.ppermute(first, axis, backward)


def shards(right_side, seam_mask, patch_inverse, row_coupling, col_coupling):
    frame_count, row_count, col_count = (lax.axis_size(axis) for axis in ("tm", "row", "col"))
    peers = row_count * col_count
    coarse_rows = 2 * row_count
    place = jnp.stack([lax.axis_index("row"), lax.axis_index("col")]).astype(jnp.int32)
    block = right_side.reshape(3, ROWS, COLS)
    mask = seam_mask.reshape(ROWS, COLS)
    last, first, middle = call(edges, [(4, RIM, COLS)] * 2 + [(4, ROWS, COLS)], "vv")(block, mask)
    low, high = exchange(last, first, "row")

    index = lax.broadcasted_iota(jnp.int32, (PATCHES, 1), 0)
    kind = index % PATCH_ROWS
    patch_row = 2 * place[0] + kind % 5 - 1
    patch_col = CELL * place[1] + index // PATCH_ROWS - 3
    kept = (kind < 15) & (kind % 5 < 4) & (patch_row >= 0) & (patch_row < coarse_rows)
    keep = (kept & (patch_col >= 0) & (patch_col < CELL * col_count)).astype(f32)

    tall, to_right, to_left, cells = call(
        assemble, [(4, TALL, LANES), (4, TALL // 2, 128), (4, TALL // 2, 128), (8, 128)], "vvv"
    )(low, middle, high)
    to_right, to_left, whole = lax.optimization_barrier((to_right, to_left, patch_inverse))
    left, right = exchange(to_right, to_left, "col")
    high_w, low_w = call(split, [(1024, 1024)] * 2, "v", limit=16, kept=bf16)(whole)
    left, right, high_w, low_w = lax.optimization_barrier((left, right, high_w, low_w))
    work = [
        pltpu.VMEM((PATCHES, 1024), bf16),
        pltpu.VMEM((PATCHES, 1024), bf16),
        pltpu.VMEM((PATCHES, 1024), f32),
    ]
    flat = pltpu.VMEM((3, FLAT, 128), f32)
    result, screen, share = call(
        functools.partial(first_apply, row_count, col_count),
        [(3, FLAT, 128), (TALL, LANES), (3 * ROWS + 8, LANES)],
        "svvvvvvv",
        [flat] + work,
        16,
    )(place, tall, left, right, cells, high_w, low_w, keep)
    before, after = exchange(share, share, "tm")
    image, last, first, message = call(
        functools.partial(first_image, peers, row_count, col_count),
        [(3, ROWS, LANES), (3, RIM, LANES), (3, RIM, LANES), (peers, 1, LANES)],
        "svvvvv",
    )(place, result, before, after, screen, cells)
    low, high = exchange(last, first, "row")
    message, row_coupling, col_coupling = lax.optimization_barrier((message, row_coupling, col_coupling))
    row_mix, row_spread, col_mix, col_spread = call(
        functools.partial(prepare, row_count, col_count),
        [(coarse_rows, coarse_rows), (SPREAD, coarse_rows), (128, 128), (128, LANES)],
        "svv",
    )(place, row_coupling, col_coupling)
    gathered = lax.all_to_all(message, ("row", "col"), 0, 0)
    first, second, partial = call(
        functools.partial(second_apply, row_count, col_count),
        [(3 * ROWS, COLS), (3 * ROWS, COLS), (1, 128)],
        "s" + "v" * 13,
        [flat] * 2 + work + [pltpu.VMEM((1024, 1024), bf16)] * 2 + [pltpu.VMEM((3, SPREAD, LANES), f32)] * 3 + [pltpu.VMEM((3, peers, 128), f32)],
        20,
    )(
        place, gathered, tall, result, image, low, high, screen, patch_inverse, keep,
        row_mix, col_mix, row_spread, col_spread,
    )
    forward = [(i, i + 1) for i in range(frame_count - 1)]
    previous = lax.ppermute(second, "tm", forward)
    group = frame_count * col_count
    (shared,) = call(functools.partial(couple, group), [(group, 1, 128)], "vvv")(second, previous, partial)
    received = lax.all_to_all(shared, ("tm", "col"), 0, 0)
    (shared,) = call(functools.partial(regroup, row_count), [(row_count, 1, 128)], "v")(received)
    received = lax.all_to_all(shared, "row", 0, 0)
    (answer,) = call(combine, [(3 * ROWS, COLS)], "vvv")(received, first, second)
    return answer.reshape(right_side.shape)


def solution(mesh):
    in_specs = (P(None, "tm", "row", "col"), P("tm", "row", "col"), P(), P(), P())
    out_specs = P(None, "tm", "row", "col")
    return jax.shard_map(shards, mesh=mesh, in_specs=in_specs, out_specs=out_specs, check_vma=False)
```
